512 devices in a mesh: rows: 32 (over z, x_hi), cols: 16 (over y, x_lo, core).
Axes of the slice: x: 4 (x_hi: 2, x_lo: 2; x = x_hi * 2 + x_lo), y: 4, z: 16, core: 2. Of those that a mesh axis runs over, the one named last changes fastest.
Arguments:
- features: bfloat16 [256, 1024, 64], P('rows', 'cols'), may hold values from -6 to 6
- hidden_prev: bfloat16 [256, 1024, 128], P('rows', 'cols'), may hold values from -6 to 6
- cell_prev: float32 [256, 1024, 128], P('rows', 'cols'), may hold values from -6 to 6
- kernel: bfloat16 [3, 3, 192, 512], replicated, may hold values from -0.15625 to 0.15625
- bias: float32 [512], replicated, may hold values from -3 to 3
- hidden_cot: bfloat16 [256, 1024, 128], P('rows', 'cols'), may hold values from -6 to 6
- cell_cot: float32 [256, 1024, 128], P('rows', 'cols'), may hold values from -6 to 6
Outputs:
- hidden_new: bfloat16 [256, 1024, 128], P('rows', 'cols')
- cell_new: float32 [256, 1024, 128], P('rows', 'cols')
- grad_features: bfloat16 [256, 1024, 64], P('rows', 'cols')
- grad_hidden: bfloat16 [256, 1024, 128], P('rows', 'cols')
- grad_cell: float32 [256, 1024, 128], P('rows', 'cols')
- grad_kernel: bfloat16 [3, 3, 192, 512], replicated
- grad_bias: float32 [512], replicated
The draws below stay inside these ranges and needn't reach their ends.
All inputs are finite; a program needn't handle non-finite values.
Results may differ from the reference program's by a relative error of at most 0.0075.
Values may be sent and summed in bfloat16 or wider, within the bound.
No kernel may reach another device: no remote copies, remote signals or barrier semaphores. Data moves between devices by JAX's collectives and lax.ppermute only.
A program may use at most 64 MiB of HBM per device.

```python
import jax
import jax.numpy as jnp
from jax import lax

CIN = 64
C = 128
NR = 256
NC = 1024
ZCH = 192
GATES = 512


def level_of(stream_key, dims, cuts, smallest, largest):
    def one(position, shards_of):
        steps = jax.random.uniform(jax.random.fold_in(jax.random.fold_in(stream_key, 6), position), (shards_of,), jnp.float32, smallest / len(cuts), largest / len(cuts))
        return jnp.repeat(jnp.exp(steps), dims[position] // shards_of).reshape((-1,) + (1,) * (len(dims) - position - 1))

    loudness = one(*cuts[0])
    for cut in cuts[1:]:
        loudness = loudness * one(*cut)
    return loudness


def noise(stream_key, dims, scale, limit, cuts=(), held_as=jnp.bfloat16):
    values = scale * jax.random.normal(stream_key, dims, jnp.float32)
    if cuts:
        values = values * level_of(stream_key, dims, cuts, -0.22, 0.18)
    return jnp.clip(values, -limit, limit).astype(held_as)


def setup_inputs(seed: int = 0) -> dict:
    seeds = jax.random.split(jax.random.key(seed), 8)
    features = noise(seeds[0], (NR, NC, CIN), 1.0, 6.0, ((0, 32), (1, 16)))
    hidden_prev = noise(seeds[1], (NR, NC, C), 1.0, 6.0, ((0, 32), (1, 16)))
    cell_prev = noise(seeds[2], (NR, NC, C), 1.0, 6.0, ((0, 32), (1, 16)), jnp.float32)
    kernel = noise(seeds[3], (3, 3, ZCH, GATES), (9 * ZCH) ** -0.5, 0.15625)
    bias = noise(seeds[4], (GATES,), 0.5, 3.0, (), jnp.float32)
    hidden_cot = noise(seeds[5], (NR, NC, C), 1.0, 6.0, ((0, 32), (1, 16)))
    cell_cot = noise(seeds[6], (NR, NC, C), 1.0, 6.0, ((0, 32), (1, 16)), jnp.float32)
    return {"features": features, "hidden_prev": hidden_prev, "cell_prev": cell_prev, "kernel": kernel, "bias": bias, "hidden_cot": hidden_cot, "cell_cot": cell_cot}


def reference(features, hidden_prev, cell_prev, kernel, bias, hidden_cot, cell_cot):
    rows_all, cols_all = features.shape[0], features.shape[1]
    zch = features.shape[2] + hidden_prev.shape[2]
    chans = hidden_prev.shape[2]
    stacked = jnp.concatenate([features, hidden_prev], axis=2)
    padded = jnp.pad(stacked, ((1, 1), (1, 1), (0, 0)))
    gates = jnp.zeros((rows_all * cols_all, 4 * chans), jnp.float32)
    for a in range(3):
        for b in range(3):
            piece = padded[a:a + rows_all, b:b + cols_all].reshape(-1, zch)
            gates = gates + jnp.dot(piece, kernel[a, b], preferred_element_type=jnp.float32)
    gates = (gates + bias).reshape(rows_all, cols_all, 4 * chans)
    in_gate = jax.nn.sigmoid(gates[..., :chans])
    forget = jax.nn.sigmoid(gates[..., chans:2 * chans])
    out_gate = jax.nn.sigmoid(gates[..., 2 * chans:3 * chans])
    cand = jnp.tanh(gates[..., 3 * chans:])
    cell_new = forget * cell_prev + in_gate * cand
    squash = jnp.tanh(cell_new)
    hidden_new = (out_gate * squash).astype(jnp.bfloat16)
    hid_cot = hidden_cot.astype(jnp.float32)
    cell_total = cell_cot + hid_cot * out_gate * (1.0 - squash * squash)
    grad_cell = cell_total * forget
    grad_gates = jnp.concatenate([
        cell_total * cand * in_gate * (1.0 - in_gate),
        cell_total * cell_prev * forget * (1.0 - forget),
        hid_cot * squash * out_gate * (1.0 - out_gate),
        cell_total * in_gate * (1.0 - cand * cand)], axis=2).astype(jnp.bfloat16)
    grad_pad = jnp.pad(grad_gates, ((1, 1), (1, 1), (0, 0)))
    flat_grad = grad_gates.reshape(-1, 4 * chans)
    grad_stacked = jnp.zeros((rows_all * cols_all, zch), jnp.float32)
    kernel_rows = []
    for a in range(3):
        for b in range(3):
            piece = grad_pad[2 - a:2 - a + rows_all, 2 - b:2 - b + cols_all].reshape(-1, 4 * chans)
            grad_stacked = grad_stacked + jnp.dot(piece, kernel[a, b].T, preferred_element_type=jnp.float32)
            source = padded[a:a + rows_all, b:b + cols_all].reshape(-1, zch)
            kernel_rows.append(lax.dot_general(source, flat_grad, (((0,), (0,)), ((), ())), preferred_element_type=jnp.float32))
    grad_stacked = grad_stacked.astype(jnp.bfloat16).reshape(rows_all, cols_all, zch)
    scale = 1.0 / rows_all
    grad_kernel = (jnp.stack(kernel_rows).reshape(3, 3, zch, 4 * chans) * scale).astype(jnp.bfloat16)
    grad_bias = jnp.sum(flat_grad.astype(jnp.float32), axis=0) * scale
    nfeat = features.shape[2]
    return (hidden_new, cell_new, grad_stacked[..., :nfeat], grad_stacked[..., nfeat:], grad_cell, grad_kernel, grad_bias)
```

```python
import jax
import jax.numpy as jnp
from jax import lax
from jax.sharding import Mesh, PartitionSpec as P

ROWS = ("z", "xh")
COLS = ("y", "xl", "core")
PLANE = ("xh", "y", "xl")
GROUP_ROWS = 216
SLOT_ROWS = 224


def with_halo(block, sides, width):
    for axis, dim in sides:
        count = lax.axis_size(axis)
        forward = [(i, i + 1) for i in range(count - 1)]
        backward = [(target, source) for source, target in forward]
        low = lax.ppermute(
            lax.slice_in_dim(block, block.shape[dim] - width, None, axis=dim), axis, forward
        )
        high = lax.ppermute(lax.slice_in_dim(block, 0, width, axis=dim), axis, backward)
        block = jnp.concatenate([low, block, high], axis=dim)
    return block


def patch_rows(padded, tile_rows, tile_cols, offsets):
    pieces = [padded[a : a + tile_rows, b : b + tile_cols] for a, b in offsets]
    return jnp.concatenate(pieces, axis=2).reshape(tile_rows * tile_cols, -1)


def spread(part, axes, count):
    copies = lax.optimization_barrier(jnp.broadcast_to(part[None], (count,) + part.shape))
    return lax.all_to_all(copies, axes, 0, 0, tiled=True)


def total_of(kernel_term, bias_term, scale):
    bf16 = jnp.bfloat16
    plane = lax.axis_size(PLANE)
    depth = lax.axis_size("z")
    groups = plane // 2
    blocks = kernel_term.reshape(groups, GROUP_ROWS, 4, 128).transpose(2, 0, 1, 3)
    extra = jnp.broadcast_to(
        bias_term.reshape(4, 1, 1, 128), (4, groups, SLOT_ROWS - GROUP_ROWS, 128)
    )
    blocks = jnp.concatenate([blocks, extra], axis=2).reshape(2, plane, SLOT_ROWS, 128)
    core = lax.axis_index("core")
    mine = lax.dynamic_index_in_dim(blocks, core, 0, keepdims=False)
    other = lax.dynamic_index_in_dim(blocks, 1 - core, 0, keepdims=False)
    half = mine + lax.ppermute(other.astype(bf16), "core", [(0, 1), (1, 0)]).astype(jnp.float32)
    part = lax.all_to_all(half.astype(bf16), PLANE, 0, 0, tiled=True)
    part = jnp.sum(part.astype(jnp.float32), axis=0).astype(bf16)
    part = lax.all_to_all(part.reshape(depth, SLOT_ROWS // depth, 128), "z", 0, 0, tiled=True)
    part = (jnp.sum(part.astype(jnp.float32), axis=0) * scale).astype(bf16)
    part = spread(part, "z", depth).reshape(SLOT_ROWS, 128)
    half = spread(part, PLANE, plane)
    whole = lax.all_gather(half, "core", axis=0).reshape(4, groups, SLOT_ROWS, 128)
    grad_kernel = whole[:, :, :GROUP_ROWS].transpose(1, 2, 0, 3).reshape(groups * GROUP_ROWS, 512)
    return grad_kernel, whole[:, 0, GROUP_ROWS].reshape(512).astype(jnp.float32)


def local(features, hidden_prev, cell_prev, kernel, bias, hidden_cot, cell_cot):
    tile_rows, tile_cols, nfeat = features.shape
    chans = hidden_prev.shape[2]
    zch = nfeat + chans
    gate_count = 4 * chans
    forward_taps = [(a, b) for a in range(3) for b in range(3)]
    stacked = jnp.concatenate([features, hidden_prev], axis=2)
    padded = with_halo(stacked, ((ROWS, 0), (COLS, 1)), 1)
    source = patch_rows(padded, tile_rows, tile_cols, forward_taps)
    gates = (
        jnp.dot(source, kernel.reshape(9 * zch, gate_count), preferred_element_type=jnp.float32)
        + bias
    )
    gates = gates.reshape(tile_rows, tile_cols, gate_count)
    in_gate = jax.nn.sigmoid(gates[..., :chans])
    forget = jax.nn.sigmoid(gates[..., chans : 2 * chans])
    out_gate = jax.nn.sigmoid(gates[..., 2 * chans : 3 * chans])
    cand = jnp.tanh(gates[..., 3 * chans :])
    cell_new = forget * cell_prev + in_gate * cand
    squash = jnp.tanh(cell_new)
    hidden_new = (out_gate * squash).astype(jnp.bfloat16)
    hid_cot = hidden_cot.astype(jnp.float32)
    cell_total = cell_cot + hid_cot * out_gate * (1.0 - squash * squash)
    grad_cell = cell_total * forget
    grad_gates = jnp.concatenate(
        [
            cell_total * cand * in_gate * (1.0 - in_gate),
            cell_total * cell_prev * forget * (1.0 - forget),
            hid_cot * squash * out_gate * (1.0 - out_gate),
            cell_total * in_gate * (1.0 - cand * cand),
        ],
        axis=2,
    ).astype(jnp.bfloat16)
    grad_pad = with_halo(grad_gates, ((ROWS, 0), (COLS, 1)), 1)
    flat_grad = grad_gates.reshape(tile_rows * tile_cols, gate_count)
    kernel_term = lax.dot_general(
        source, flat_grad, (((0,), (0,)), ((), ())), preferred_element_type=jnp.float32
    )
    bias_term = jnp.sum(flat_grad.astype(jnp.float32), axis=0)[None, :]
    flipped = jnp.transpose(kernel[::-1, ::-1], (0, 1, 3, 2)).reshape(9 * gate_count, zch)
    grad_source = patch_rows(grad_pad, tile_rows, tile_cols, forward_taps)
    grad_stacked = jnp.dot(grad_source, flipped, preferred_element_type=jnp.float32)
    grad_stacked = grad_stacked.astype(jnp.bfloat16).reshape(tile_rows, tile_cols, zch)
    scale = 1.0 / (tile_rows * lax.axis_size(ROWS))
    grad_kernel, grad_bias = total_of(kernel_term, bias_term, scale)
    return (
        hidden_new,
        cell_new,
        grad_stacked[..., :nfeat],
        grad_stacked[..., nfeat:],
        grad_cell,
        grad_kernel.reshape(3, 3, zch, gate_count),
        grad_bias,
    )


def solution(mesh):
    grid = Mesh(mesh.devices.reshape(16, 2, 4, 2, 2), ROWS + COLS)
    tile = P(ROWS, COLS, None)
    return jax.shard_map(
        local,
        mesh=grid,
        in_specs=(tile, tile, tile, P(), P(), tile, tile),
        out_specs=(tile, tile, tile, tile, tile, P(), P()),
        check_vma=False,
    )
```

```python
import jax
import jax.numpy as jnp
from jax import lax
from jax.sharding import Mesh, PartitionSpec as P

ROWS = ("z", "xh")
COLS = ("y", "xl", "core")
PLANE = ("xh", "y", "xl")
GROUP_ROWS = 216
SLOT_ROWS = 224


def with_halo(block, sides, width):
    for axis, dim in sides:
        count = lax.axis_size(axis)
        forward = [(i, i + 1) for i in range(count - 1)]
        backward = [(target, source) for source, target in forward]
        low = lax.ppermute(
            lax.slice_in_dim(block, block.shape[dim] - width, None, axis=dim), axis, forward
        )
        high = lax.ppermute(lax.slice_in_dim(block, 0, width, axis=dim), axis, backward)
        block = jnp.concatenate([low, block, high], axis=dim)
    return block


def patch_rows(padded, tile_rows, tile_cols, offsets):
    pieces = [padded[a : a + tile_rows, b : b + tile_cols] for a, b in offsets]
    return jnp.concatenate(pieces, axis=2).reshape(tile_rows * tile_cols, -1)


def spread(part, axes, count):
    copies = lax.optimization_barrier(jnp.broadcast_to(part[None], (count,) + part.shape))
    return lax.all_to_all(copies, axes, 0, 0, tiled=True)


def total_of(kernel_term, bias_term, scale):
    bf16 = jnp.bfloat16
    plane = lax.axis_size(PLANE)
    depth = lax.axis_size("z")
    groups = plane // 2
    blocks = kernel_term.reshape(groups, GROUP_ROWS, 4, 128).transpose(2, 0, 1, 3)
    extra = jnp.broadcast_to(
        bias_term.reshape(4, 1, 1, 128), (4, groups, SLOT_ROWS - GROUP_ROWS, 128)
    )
    blocks = jnp.concatenate([blocks, extra], axis=2).reshape(2, plane, SLOT_ROWS, 128)
    core = lax.axis_index("core")
    mine = lax.dynamic_index_in_dim(blocks, core, 0, keepdims=False)
    other = lax.dynamic_index_in_dim(blocks, 1 - core, 0, keepdims=False)
    half = mine + lax.ppermute(other.astype(bf16), "core", [(0, 1), (1, 0)]).astype(jnp.float32)
    part = lax.all_to_all(half.astype(bf16), PLANE, 0, 0, tiled=True)
    part = jnp.sum(part.astype(jnp.float32), axis=0).astype(bf16)
    part = lax.all_to_all(part.reshape(depth, SLOT_ROWS // depth, 128), "z", 0, 0, tiled=True)
    part = (jnp.sum(part.astype(jnp.float32), axis=0) * scale).astype(bf16)
    part = spread(part, "z", depth).reshape(SLOT_ROWS, 128)
    half = spread(part, PLANE, plane)
    swapped = lax.ppermute(half, "core", [(0, 1), (1, 0)])
    first = jnp.where(core == 0, half, swapped)
    second = jnp.where(core == 0, swapped, half)
    whole = jnp.stack([first, second]).reshape(4, groups, SLOT_ROWS, 128)
    grad_kernel = whole[:, :, :GROUP_ROWS].transpose(1, 2, 0, 3).reshape(groups * GROUP_ROWS, 512)
    return grad_kernel, whole[:, 0, GROUP_ROWS].reshape(512).astype(jnp.float32)


def local(features, hidden_prev, cell_prev, kernel, bias, hidden_cot, cell_cot):
    tile_rows, tile_cols, nfeat = features.shape
    chans = hidden_prev.shape[2]
    zch = nfeat + chans
    gate_count = 4 * chans
    forward_taps = [(a, b) for a in range(3) for b in range(3)]
    stacked = jnp.concatenate([features, hidden_prev], axis=2)
    padded = with_halo(stacked, ((ROWS, 0), (COLS, 1)), 1)
    source = patch_rows(padded, tile_rows, tile_cols, forward_taps)
    gates = (
        jnp.dot(source, kernel.reshape(9 * zch, gate_count), preferred_element_type=jnp.float32)
        + bias
    )
    gates = gates.reshape(tile_rows, tile_cols, gate_count)
    in_gate = jax.nn.sigmoid(gates[..., :chans])
    forget = jax.nn.sigmoid(gates[..., chans : 2 * chans])
    out_gate = jax.nn.sigmoid(gates[..., 2 * chans : 3 * chans])
    cand = jnp.tanh(gates[..., 3 * chans :])
    cell_new = forget * cell_prev + in_gate * cand
    squash = jnp.tanh(cell_new)
    hidden_new = (out_gate * squash).astype(jnp.bfloat16)
    hid_cot = hidden_cot.astype(jnp.float32)
    cell_total = cell_cot + hid_cot * out_gate * (1.0 - squash * squash)
    grad_cell = cell_total * forget
    grad_gates = jnp.concatenate(
        [
            cell_total * cand * in_gate * (1.0 - in_gate),
            cell_total * cell_prev * forget * (1.0 - forget),
            hid_cot * squash * out_gate * (1.0 - out_gate),
            cell_total * in_gate * (1.0 - cand * cand),
        ],
        axis=2,
    ).astype(jnp.bfloat16)
    grad_pad = with_halo(grad_gates, ((ROWS, 0), (COLS, 1)), 1)
    flat_grad = grad_gates.reshape(tile_rows * tile_cols, gate_count)
    kernel_term = lax.dot_general(
        source, flat_grad, (((0,), (0,)), ((), ())), preferred_element_type=jnp.float32
    )
    bias_term = jnp.sum(flat_grad.astype(jnp.float32), axis=0)[None, :]
    flipped = jnp.transpose(kernel[::-1, ::-1], (0, 1, 3, 2)).reshape(9 * gate_count, zch)
    grad_source = patch_rows(grad_pad, tile_rows, tile_cols, forward_taps)
    grad_stacked = jnp.dot(grad_source, flipped, preferred_element_type=jnp.float32)
    grad_stacked = grad_stacked.astype(jnp.bfloat16).reshape(tile_rows, tile_cols, zch)
    scale = 1.0 / (tile_rows * lax.axis_size(ROWS))
    grad_kernel, grad_bias = total_of(kernel_term, bias_term, scale)
    return (
        hidden_new,
        cell_new,
        grad_stacked[..., :nfeat],
        grad_stacked[..., nfeat:],
        grad_cell,
        grad_kernel.reshape(3, 3, zch, gate_count),
        grad_bias,
    )


def solution(mesh):
    grid = Mesh(mesh.devices.reshape(16, 2, 4, 2, 2), ROWS + COLS)
    tile = P(ROWS, COLS, None)
    return jax.shard_map(
        local,
        mesh=grid,
        in_specs=(tile, tile, tile, P(), P(), tile, tile),
        out_specs=(tile, tile, tile, tile, tile, P(), P()),
        check_vma=False,
    )
```

```python
import jax
import jax.numpy as jnp
from jax import lax
from jax.experimental import pallas as pl
from jax.experimental.pallas import tpu as pltpu
from jax.sharding import Mesh, PartitionSpec as P

ROWS = ("z", "xh")
COLS = ("y", "xl", "core")
PLANE = ("xh", "y", "xl")
BF16 = jnp.bfloat16
F32 = jnp.float32
TR, TC = 8, 64
CELLS = TR * TC
FEAT, CH, ZCH, GATES = 64, 128, 192, 512
TAPS = 3 * ZCH
GROUPS, SLOT = 8, 224
VMEM = 40 * 1024 * 1024


def halo_rows(block):
    count = lax.axis_size(ROWS)
    forward = [(i, i + 1) for i in range(count - 1)]
    backward = [(target, source) for source, target in forward]
    low = lax.ppermute(block[TR - 1 :], ROWS, forward)
    high = lax.ppermute(block[:1], ROWS, backward)
    return low, high


def halo_cols(low, block, high):
    count = lax.axis_size(COLS)
    forward = [(i, i + 1) for i in range(count - 1)]
    backward = [(target, source) for source, target in forward]
    last = jnp.concatenate([low[:, TC - 1 :], block[:, TC - 1 :], high[:, TC - 1 :]], axis=0)
    first = jnp.concatenate([low[:, :1], block[:, :1], high[:, :1]], axis=0)
    return lax.ppermute(last, COLS, forward), lax.ppermute(first, COLS, backward)


def shifted(row, before, after):
    place = lax.broadcasted_iota(jnp.int32, row.shape, 0)
    down = jnp.where(place == 0, before, pltpu.roll(row, 1, 0))
    up = jnp.where(place == TC - 1, after, pltpu.roll(row, TC - 1, 0))
    return down, up


def taps_kernel(stacked, taps):
    for r in range(TR):
        row = stacked[r].astype(F32)
        down, up = shifted(row, 0.0, 0.0)
        taps[(r + 1) * TC : (r + 2) * TC, :] = jnp.concatenate([down, row, up], axis=1).astype(BF16)


def half_products(taps, half_gates, half_bias, store):
    for a in range(3):
        term = lax.dot_general(
            taps[a * TC : a * TC + CELLS, :],
            half_gates,
            (((0,), (0,)), ((), ())),
            preferred_element_type=F32,
        )
        begin = a * TAPS
        while begin < (a + 1) * TAPS:
            end = min((begin // SLOT + 1) * SLOT, (a + 1) * TAPS)
            group, top = begin // SLOT, begin % SLOT
            for j in range(2):
                block = term[begin - a * TAPS : end - a * TAPS, j * 128 : (j + 1) * 128]
                store(j * GROUPS + group, top, top + end - begin, block)
            begin = end
    top = 3 * TAPS - (GROUPS - 1) * SLOT
    for j in range(2):
        slot = j * GROUPS + GROUPS - 1
        row = half_bias[:, j * 128 : (j + 1) * 128]
        store(slot, top, top + 16, jnp.concatenate([row, row], axis=0))
        store(slot, top + 16, SLOT, jnp.zeros((SLOT - top - 16, 128), F32))


def cell_kernel(
    own_taps, low, high, left, right, kernel, cell_prev, hidden_cot, cell_cot, bias,
    hidden_new, cell_new, grad_cell, grad_gates, taps, sums, send, gates,
):
    for r, halo in ((0, low), (TR + 1, high)):
        row = halo[0].astype(F32)
        down, up = shifted(row, left[r].astype(F32), right[r].astype(F32))
        taps[r * TC : (r + 1) * TC, :] = jnp.concatenate([down, row, up], axis=1).astype(BF16)
    place = lax.broadcasted_iota(jnp.int32, (16, ZCH), 0)
    for r in range(1, TR + 1):
        begin, end = r * TC, (r + 1) * TC
        taps[begin + 16 : end - 16, :] = own_taps[begin + 16 : end - 16, :]
        block = own_taps[begin : begin + 16, :].astype(F32)
        side = jnp.where(place == 0, left[r].astype(F32), block[:, :ZCH])
        taps[begin : begin + 16, :] = jnp.concatenate([side, block[:, ZCH:]], axis=1).astype(BF16)
        block = own_taps[end - 16 : end, :].astype(F32)
        side = jnp.where(place == 15, right[r].astype(F32), block[:, 2 * ZCH :])
        taps[end - 16 : end, :] = jnp.concatenate([block[:, : 2 * ZCH], side], axis=1).astype(BF16)
    total = jnp.dot(taps[0:CELLS, :], kernel[0], preferred_element_type=F32)
    total += jnp.dot(taps[TC : TC + CELLS, :], kernel[1], preferred_element_type=F32)
    total += jnp.dot(taps[2 * TC : 2 * TC + CELLS, :], kernel[2], preferred_element_type=F32)
    gates[...] = total + bias[...]
    bias_sum = jnp.zeros((8, GATES), F32)
    for r in range(TR):
        rows = slice(r * TC, (r + 1) * TC)
        in_gate = jax.nn.sigmoid(gates[rows, 0:CH])
        forget = jax.nn.sigmoid(gates[rows, CH : 2 * CH])
        out_gate = jax.nn.sigmoid(gates[rows, 2 * CH : 3 * CH])
        cand = jnp.tanh(gates[rows, 3 * CH :])
        before = cell_prev[r]
        new = forget * before + in_gate * cand
        squash = jnp.tanh(new)
        cell_new[r] = new
        hidden_new[r] = (out_gate * squash).astype(BF16)
        hid_cot = hidden_cot[r].astype(F32)
        total = cell_cot[r] + hid_cot * out_gate * (1.0 - squash * squash)
        grad_cell[r] = total * forget
        parts = [
            total * cand * in_gate * (1.0 - in_gate),
            total * before * forget * (1.0 - forget),
            hid_cot * squash * out_gate * (1.0 - out_gate),
            total * in_gate * (1.0 - cand * cand),
        ]
        rounded = jnp.concatenate([part.astype(BF16) for part in parts], axis=1)
        grad_gates[rows, :] = rounded
        wide = rounded.astype(F32).reshape(TC // 8, 8, GATES)
        bias_sum = bias_sum + jnp.sum(wide, axis=0)
    sums[...] = jnp.broadcast_to(jnp.sum(bias_sum, axis=0, keepdims=True), (8, GATES))
    columns = pl.ds(pl.multiple_of((1 - lax.axis_index("core")) * 256, 256), 256)

    def store(slot, top, end, block):
        send[slot, top:end, :] = block.astype(BF16)

    half_products(taps, grad_gates[:, columns], sums[:, columns], store)


def own_kernel(taps, grad_gates, sums, received, total):
    columns = pl.ds(pl.multiple_of(lax.axis_index("core") * 256, 256), 256)

    def store(slot, top, end, block):
        total[slot, top:end, :] = (block + received[slot, top:end, :].astype(F32)).astype(BF16)

    half_products(taps, grad_gates[:, columns], sums[:, columns], store)


def input_kernel(
    grad_gates, low, high, left, right, kernel, grad_features, grad_hidden, moved, result
):
    for r in range(TR + 2):
        if r == 0:
            row = low[0]
        elif r == TR + 1:
            row = high[0]
        else:
            row = grad_gates[(r - 1) * TC : r * TC, :]
        rows = slice(r * TC, (r + 1) * TC)
        down, up = shifted(row.astype(F32), left[r].astype(F32), right[r].astype(F32))
        moved[0, rows, :] = down.astype(BF16)
        moved[1, rows, :] = row
        moved[2, rows, :] = up.astype(BF16)
    for tap in range(9):
        a, b = tap // 3, tap % 3
        term = lax.dot_general(
            moved[2 - b, (2 - a) * TC : (2 - a) * TC + CELLS, :],
            kernel[a, b * ZCH : (b + 1) * ZCH, :],
            (((1,), (1,)), ((), ())),
            preferred_element_type=F32,
        )
        if tap == 0:
            result[...] = term
        else:
            result[...] += term
    for r in range(TR):
        block = result[r * TC : (r + 1) * TC, :]
        grad_features[r] = block[:, :FEAT].astype(BF16)
        grad_hidden[r] = block[:, FEAT:].astype(BF16)


def join_kernel(own, other, grad_kernel, grad_bias):
    core = lax.axis_index("core")
    last = 3 * TAPS - (GROUPS - 1) * SLOT
    for source, place in ((own, core), (other, 1 - core)):
        for j in range(2):
            columns = pl.ds(pl.multiple_of(place * 256 + j * 128, 128), 128)
            for i in range(GROUPS):
                count = SLOT if i < GROUPS - 1 else last
                grad_kernel[i * SLOT : i * SLOT + count, columns] = source[
                    j * GROUPS + i, 0:count, :
                ]
            row = source[j * GROUPS + GROUPS - 1, last : last + 16, :].astype(F32)
            grad_bias[:, columns] = row[0:1]


def call(body, outs, *args, scratch=(), flops=0):
    moved = sum(x.size * x.dtype.itemsize for x in list(args) + list(outs))
    whole = pl.BlockSpec(memory_space=pltpu.VMEM)
    return pl.pallas_call(
        body,
        out_shape=outs,
        in_specs=[whole] * len(args),
        out_specs=[whole] * len(outs),
        scratch_shapes=list(scratch),
        cost_estimate=pl.CostEstimate(flops=flops, bytes_accessed=moved, transcendentals=0),
        compiler_params=pltpu.CompilerParams(vmem_limit_bytes=VMEM),
    )(*args)


def copies_of(part, count):
    return lax.optimization_barrier(jnp.broadcast_to(part[None], (count,) + part.shape))


def local(features, hidden_prev, cell_prev, kernel, bias, hidden_cot, cell_cot):
    shape = jax.ShapeDtypeStruct
    work = 2 * CELLS * 3 * TAPS * GATES
    plane = lax.axis_size(PLANE)
    depth = lax.axis_size("z")
    swap = [(0, 1), (1, 0)]
    weights = kernel.reshape(3, TAPS, GATES)

    stacked = jnp.concatenate([features, hidden_prev], axis=2)
    low, high = halo_rows(stacked)
    (own_taps,) = call(
        taps_kernel, (shape(((TR + 2) * TC, TAPS), BF16),), stacked, flops=work
    )
    low, high, own_taps = lax.optimization_barrier((low, high, own_taps))
    left, right = halo_cols(low, stacked, high)
    hidden_new, cell_new, grad_cell, grad_gates, taps, sums, send = call(
        cell_kernel,
        (
            shape((TR, TC, CH), BF16),
            shape((TR, TC, CH), F32),
            shape((TR, TC, CH), F32),
            shape((CELLS, GATES), BF16),
            shape(((TR + 2) * TC, TAPS), BF16),
            shape((8, GATES), F32),
            shape((plane, SLOT, 128), BF16),
        ),
        own_taps, low, high, left, right, weights, cell_prev, hidden_cot, cell_cot,
        bias.reshape(1, GATES),
        scratch=[pltpu.VMEM((CELLS, GATES), F32)],
        flops=work + work // 2,
    )
    received = lax.ppermute(send, "core", swap)
    gate_tile = grad_gates.reshape(TR, TC, GATES)
    gate_low, gate_high = halo_rows(gate_tile)
    (half,) = call(
        own_kernel, (shape((plane, SLOT, 128), BF16),), taps, grad_gates, sums, received,
        flops=work // 2,
    )
    half, gate_low, gate_high = lax.optimization_barrier((half, gate_low, gate_high))
    part = lax.all_to_all(half, PLANE, 0, 0, tiled=True)
    part = jnp.sum(part.astype(F32), axis=0).astype(BF16)
    part = lax.all_to_all(part.reshape(depth, SLOT // depth, 128), "z", 0, 0, tiled=True)
    scale = 1.0 / (TR * lax.axis_size(ROWS))
    part = (jnp.sum(part.astype(F32), axis=0) * scale).astype(BF16)
    part = lax.all_to_all(copies_of(part, depth), "z", 0, 0, tiled=True).reshape(SLOT, 128)
    copies, gate_low, gate_tile, gate_high = lax.optimization_barrier(
        (copies_of(part, plane), gate_low, gate_tile, gate_high)
    )
    half = lax.all_to_all(copies, PLANE, 0, 0, tiled=True)
    gate_left, gate_right = halo_cols(gate_low, gate_tile, gate_high)
    grad_features, grad_hidden = call(
        input_kernel,
        (shape((TR, TC, FEAT), BF16), shape((TR, TC, CH), BF16)),
        grad_gates, gate_low, gate_high, gate_left, gate_right, weights,
        scratch=[pltpu.VMEM((3, (TR + 2) * TC, GATES), BF16), pltpu.VMEM((CELLS, ZCH), F32)],
        flops=work,
    )
    half, grad_features, grad_hidden = lax.optimization_barrier(
        (half, grad_features, grad_hidden)
    )
    other = lax.ppermute(half, "core", swap)
    grad_kernel, grad_bias = call(
        join_kernel, (shape((3 * TAPS, GATES), BF16), shape((1, GATES), F32)), half, other
    )
    return (
        hidden_new,
        cell_new,
        grad_features,
        grad_hidden,
        grad_cell,
        grad_kernel.reshape(3, 3, ZCH, GATES),
        grad_bias.reshape(GATES),
    )


def solution(mesh):
    grid = Mesh(mesh.devices.reshape(16, 2, 4, 2, 2), ROWS + COLS)
    tile = P(ROWS, COLS, None)
    return jax.shard_map(
        local,
        mesh=grid,
        in_specs=(tile, tile, tile, P(), P(), tile, tile),
        out_specs=(tile, tile, tile, tile, tile, P(), P()),
        check_vma=False,
    )
```

```python
import jax
import jax.numpy as jnp
from jax import lax
from jax.experimental import pallas as pl
from jax.experimental.pallas import tpu as pltpu
from jax.sharding import Mesh, PartitionSpec as P

ROWS = ("z", "xh")
COLS = ("y", "xl", "core")
PLANE = ("xh", "y", "xl")
BF16 = jnp.bfloat16
F32 = jnp.float32
TR, TC = 8, 64
CELLS = TR * TC
FEAT, CH, ZCH, GATES = 64, 128, 192, 512
TAPS = 3 * ZCH
GROUPS, SLOT = 8, 224
VMEM = 40 * 1024 * 1024


def halo_rows(block):
    count = lax.axis_size(ROWS)
    forward = [(i, i + 1) for i in range(count - 1)]
    backward = [(target, source) for source, target in forward]
    low = lax.ppermute(block[TR - 1 :], ROWS, forward)
    high = lax.ppermute(block[:1], ROWS, backward)
    return low, high


def halo_cols(low, block, high):
    count = lax.axis_size(COLS)
    forward = [(i, i + 1) for i in range(count - 1)]
    backward = [(target, source) for source, target in forward]
    last = jnp.concatenate([low[:, TC - 1 :], block[:, TC - 1 :], high[:, TC - 1 :]], axis=0)
    first = jnp.concatenate([low[:, :1], block[:, :1], high[:, :1]], axis=0)
    return lax.ppermute(last, COLS, forward), lax.ppermute(first, COLS, backward)


def shifted(row, before, after):
    place = lax.broadcasted_iota(jnp.int32, row.shape, 0)
    down = jnp.where(place == 0, before, pltpu.roll(row, 1, 0))
    up = jnp.where(place == TC - 1, after, pltpu.roll(row, TC - 1, 0))
    return down, up


def taps_kernel(stacked, taps):
    for r in range(TR):
        row = stacked[r].astype(F32)
        down, up = shifted(row, 0.0, 0.0)
        taps[(r + 1) * TC : (r + 2) * TC, :] = jnp.concatenate([down, row, up], axis=1).astype(BF16)


def half_products(taps, half_gates, half_bias, store, finish=lambda slot: None):
    for a in range(3):
        term = lax.dot_general(
            taps[a * TC : a * TC + CELLS, :],
            half_gates,
            (((0,), (0,)), ((), ())),
            preferred_element_type=F32,
        )
        begin = a * TAPS
        while begin < (a + 1) * TAPS:
            end = min((begin // SLOT + 1) * SLOT, (a + 1) * TAPS)
            group, top = begin // SLOT, begin % SLOT
            for j in range(2):
                block = term[begin - a * TAPS : end - a * TAPS, j * 128 : (j + 1) * 128]
                store(j * GROUPS + group, top, top + end - begin, block)
                if end % SLOT == 0:
                    finish(j * GROUPS + group)
            begin = end
    top = 3 * TAPS - (GROUPS - 1) * SLOT
    for j in range(2):
        slot = j * GROUPS + GROUPS - 1
        row = half_bias[:, j * 128 : (j + 1) * 128]
        store(slot, top, top + 16, jnp.concatenate([row, row], axis=0))
        store(slot, top + 16, SLOT, jnp.zeros((SLOT - top - 16, 128), F32))
        finish(slot)


def cell_kernel(
    own_taps, low, high, left, right, kernel, cell_prev, hidden_cot, cell_cot, bias,
    hidden_new, cell_new, grad_cell, grad_gates, taps, sums, send, gates,
):
    for r, halo in ((0, low), (TR + 1, high)):
        row = halo[0].astype(F32)
        down, up = shifted(row, left[r].astype(F32), right[r].astype(F32))
        taps[r * TC : (r + 1) * TC, :] = jnp.concatenate([down, row, up], axis=1).astype(BF16)
    place = lax.broadcasted_iota(jnp.int32, (16, ZCH), 0)
    for r in range(1, TR + 1):
        begin, end = r * TC, (r + 1) * TC
        taps[begin + 16 : end - 16, :] = own_taps[begin + 16 : end - 16, :]
        block = own_taps[begin : begin + 16, :].astype(F32)
        side = jnp.where(place == 0, left[r].astype(F32), block[:, :ZCH])
        taps[begin : begin + 16, :] = jnp.concatenate([side, block[:, ZCH:]], axis=1).astype(BF16)
        block = own_taps[end - 16 : end, :].astype(F32)
        side = jnp.where(place == 15, right[r].astype(F32), block[:, 2 * ZCH :])
        taps[end - 16 : end, :] = jnp.concatenate([block[:, : 2 * ZCH], side], axis=1).astype(BF16)
    total = jnp.dot(taps[0:CELLS, :], kernel[0], preferred_element_type=F32)
    total += jnp.dot(taps[TC : TC + CELLS, :], kernel[1], preferred_element_type=F32)
    total += jnp.dot(taps[2 * TC : 2 * TC + CELLS, :], kernel[2], preferred_element_type=F32)
    gates[...] = total + bias[...]
    bias_sum = jnp.zeros((8, GATES), F32)
    for r in range(TR):
        rows = slice(r * TC, (r + 1) * TC)
        in_gate = jax.nn.sigmoid(gates[rows, 0:CH])
        forget = jax.nn.sigmoid(gates[rows, CH : 2 * CH])
        out_gate = jax.nn.sigmoid(gates[rows, 2 * CH : 3 * CH])
        cand = jnp.tanh(gates[rows, 3 * CH :])
        before = cell_prev[r]
        new = forget * before + in_gate * cand
        squash = jnp.tanh(new)
        cell_new[r] = new
        hidden_new[r] = (out_gate * squash).astype(BF16)
        hid_cot = hidden_cot[r].astype(F32)
        total = cell_cot[r] + hid_cot * out_gate * (1.0 - squash * squash)
        grad_cell[r] = total * forget
        parts = [
            total * cand * in_gate * (1.0 - in_gate),
            total * before * forget * (1.0 - forget),
            hid_cot * squash * out_gate * (1.0 - out_gate),
            total * in_gate * (1.0 - cand * cand),
        ]
        rounded = jnp.concatenate([part.astype(BF16) for part in parts], axis=1)
        grad_gates[rows, :] = rounded
        wide = rounded.astype(F32).reshape(TC // 8, 8, GATES)
        bias_sum = bias_sum + jnp.sum(wide, axis=0)
    sums[...] = jnp.broadcast_to(jnp.sum(bias_sum, axis=0, keepdims=True), (8, GATES))
    columns = pl.ds(pl.multiple_of((1 - lax.axis_index("core")) * 256, 256), 256)

    def store(slot, top, end, block):
        send[slot, top:end, :] = block.astype(BF16)

    half_products(taps, grad_gates[:, columns], sums[:, columns], store)


def own_kernel(taps, grad_gates, sums, received, result, total, sent):
    columns = pl.ds(pl.multiple_of(lax.axis_index("core") * 256, 256), 256)

    def store(slot, top, end, block):
        total[slot, top:end, :] = (block + received[slot, top:end, :].astype(F32)).astype(BF16)

    def copy(slot):
        return pltpu.make_async_copy(total.at[slot], result.at[slot], sent.at[slot])

    half_products(
        taps, grad_gates[:, columns], sums[:, columns], store, lambda slot: copy(slot).start()
    )
    for slot in range(2 * GROUPS):
        copy(slot).wait()


def input_kernel(
    grad_gates, low, high, left, right, kernel, grad_features, grad_hidden, moved, result
):
    for r in range(TR + 2):
        if r == 0:
            row = low[0]
        elif r == TR + 1:
            row = high[0]
        else:
            row = grad_gates[(r - 1) * TC : r * TC, :]
        rows = slice(r * TC, (r + 1) * TC)
        down, up = shifted(row.astype(F32), left[r].astype(F32), right[r].astype(F32))
        moved[0, rows, :] = down.astype(BF16)
        moved[1, rows, :] = row
        moved[2, rows, :] = up.astype(BF16)
    for tap in range(9):
        a, b = tap // 3, tap % 3
        term = lax.dot_general(
            moved[2 - b, (2 - a) * TC : (2 - a) * TC + CELLS, :],
            kernel[a, b * ZCH : (b + 1) * ZCH, :],
            (((1,), (1,)), ((), ())),
            preferred_element_type=F32,
        )
        if tap == 0:
            result[...] = term
        else:
            result[...] += term
    for r in range(TR):
        block = result[r * TC : (r + 1) * TC, :]
        grad_features[r] = block[:, :FEAT].astype(BF16)
        grad_hidden[r] = block[:, FEAT:].astype(BF16)


def place_half(slots, place, grad_kernel, grad_bias, last_slots, sems):
    last = 3 * TAPS - (GROUPS - 1) * SLOT
    copies = []
    for j in range(2):
        columns = pl.ds(pl.multiple_of(place * 256 + j * 128, 128), 128)
        slot = j * GROUPS + GROUPS - 1
        copies.append(
            pltpu.make_async_copy(
                slots.at[slot, last : last + 16, :], last_slots.at[j], sems.at[2 * GROUPS + j]
            )
        )
        for i in range(GROUPS):
            count = SLOT if i < GROUPS - 1 else last
            copies.append(
                pltpu.make_async_copy(
                    slots.at[j * GROUPS + i, 0:count, :],
                    grad_kernel.at[i * SLOT : i * SLOT + count, columns],
                    sems.at[j * GROUPS + i],
                )
            )
    for copy in copies:
        copy.start()
    for copy in copies:
        copy.wait()
    for j in range(2):
        columns = pl.ds(pl.multiple_of(place * 256 + j * 128, 128), 128)
        grad_bias[:, columns] = last_slots[j].astype(F32)[0:1]


def join_own_kernel(slots, grad_kernel, grad_bias, last_slots, sems):
    grad_bias[...] = jnp.zeros_like(grad_bias)
    place_half(slots, lax.axis_index("core"), grad_kernel, grad_bias, last_slots, sems)


def join_other_kernel(
    own_bias, slots, own_kernel_part, grad_kernel, grad_bias, last_slots, sems
):
    grad_bias[...] = own_bias[...]
    place_half(slots, 1 - lax.axis_index("core"), grad_kernel, grad_bias, last_slots, sems)


def call(body, outs, *args, scratch=(), flops=0, far=0, far_outs=0, aliases=()):
    moved = sum(x.size * x.dtype.itemsize for x in list(args) + list(outs))
    whole = pl.BlockSpec(memory_space=pltpu.VMEM)
    anywhere = pl.BlockSpec(memory_space=pl.ANY)
    return pl.pallas_call(
        body,
        out_shape=outs,
        in_specs=[whole] * (len(args) - far) + [anywhere] * far,
        out_specs=[anywhere] * far_outs + [whole] * (len(outs) - far_outs),
        input_output_aliases=dict(aliases),
        scratch_shapes=list(scratch),
        cost_estimate=pl.CostEstimate(flops=flops, bytes_accessed=moved, transcendentals=0),
        compiler_params=pltpu.CompilerParams(vmem_limit_bytes=VMEM),
    )(*args)


def copies_of(part, count):
    return lax.optimization_barrier(jnp.broadcast_to(part[None], (count,) + part.shape))


def local(features, hidden_prev, cell_prev, kernel, bias, hidden_cot, cell_cot):
    shape = jax.ShapeDtypeStruct
    work = 2 * CELLS * 3 * TAPS * GATES
    plane = lax.axis_size(PLANE)
    depth = lax.axis_size("z")
    swap = [(0, 1), (1, 0)]
    weights = kernel.reshape(3, TAPS, GATES)

    stacked = jnp.concatenate([features, hidden_prev], axis=2)
    low, high = halo_rows(stacked)
    (own_taps,) = call(
        taps_kernel, (shape(((TR + 2) * TC, TAPS), BF16),), stacked, flops=work
    )
    low, high, own_taps = lax.optimization_barrier((low, high, own_taps))
    left, right = halo_cols(low, stacked, high)
    hidden_new, cell_new, grad_cell, grad_gates, taps, sums, send = call(
        cell_kernel,
        (
            shape((TR, TC, CH), BF16),
            shape((TR, TC, CH), F32),
            shape((TR, TC, CH), F32),
            shape((CELLS, GATES), BF16),
            shape(((TR + 2) * TC, TAPS), BF16),
            shape((8, GATES), F32),
            shape((plane, SLOT, 128), BF16),
        ),
        own_taps, low, high, left, right, weights, cell_prev, hidden_cot, cell_cot,
        bias.reshape(1, GATES),
        scratch=[pltpu.VMEM((CELLS, GATES), F32)],
        flops=work + work // 2,
    )
    received = lax.ppermute(send, "core", swap)
    (half,) = call(
        own_kernel, (shape((plane, SLOT, 128), BF16),), taps, grad_gates, sums, received,
        scratch=[pltpu.VMEM((plane, SLOT, 128), BF16), pltpu.SemaphoreType.DMA((plane,))],
        flops=work // 2,
        far_outs=1,
    )
    half, gate_tile = lax.optimization_barrier((half, grad_gates.reshape(TR, TC, GATES)))
    part = lax.all_to_all(half, PLANE, 0, 0, tiled=True)
    gate_low, gate_high = halo_rows(gate_tile)
    part, gate_low, gate_high = lax.optimization_barrier((part, gate_low, gate_high))
    part = jnp.sum(part.astype(F32), axis=0).astype(BF16)
    part = lax.all_to_all(part.reshape(depth, SLOT // depth, 128), "z", 0, 0, tiled=True)
    scale = 1.0 / (TR * lax.axis_size(ROWS))
    part = (jnp.sum(part.astype(F32), axis=0) * scale).astype(BF16)
    part = lax.all_to_all(copies_of(part, depth), "z", 0, 0, tiled=True).reshape(SLOT, 128)
    copies, gate_low, gate_tile, gate_high = lax.optimization_barrier(
        (copies_of(part, plane), gate_low, gate_tile, gate_high)
    )
    half = lax.all_to_all(copies, PLANE, 0, 0, tiled=True)
    gate_left, gate_right = halo_cols(gate_low, gate_tile, gate_high)
    grad_features, grad_hidden = call(
        input_kernel,
        (shape((TR, TC, FEAT), BF16), shape((TR, TC, CH), BF16)),
        grad_gates, gate_low, gate_high, gate_left, gate_right, weights,
        scratch=[pltpu.VMEM((3, (TR + 2) * TC, GATES), BF16), pltpu.VMEM((CELLS, ZCH), F32)],
        flops=work,
    )
    half, grad_features, grad_hidden = lax.optimization_barrier(
        (half, grad_features, grad_hidden)
    )
    other = lax.ppermute(half, "core", swap)
    outs = (shape((3 * TAPS, GATES), BF16), shape((1, GATES), F32))
    scratch = [pltpu.VMEM((2, 16, 128), BF16), pltpu.SemaphoreType.DMA((2 * GROUPS + 2,))]
    grad_kernel, own_bias = call(
        join_own_kernel, outs, half, scratch=scratch, far=1, far_outs=1
    )
    grad_kernel, grad_bias = call(
        join_other_kernel, outs, own_bias, other, grad_kernel,
        scratch=scratch, far=2, far_outs=1, aliases={2: 0},
    )
    return (
        hidden_new,
        cell_new,
        grad_features,
        grad_hidden,
        grad_cell,
        grad_kernel.reshape(3, 3, ZCH, GATES),
        grad_bias.reshape(GATES),
    )


def solution(mesh):
    grid = Mesh(mesh.devices.reshape(16, 2, 4, 2, 2), ROWS + COLS)
    tile = P(ROWS, COLS, None)
    return jax.shard_map(
        local,
        mesh=grid,
        in_specs=(tile, tile, tile, P(), P(), tile, tile),
        out_specs=(tile, tile, tile, tile, tile, P(), P()),
        check_vma=False,
    )
```

```python
import jax
import jax.numpy as jnp
from jax import lax
from jax.experimental import pallas as pl
from jax.experimental.pallas import tpu as pltpu
from jax.sharding import Mesh, PartitionSpec as P

ROWS = ("z", "xh")
COLS = ("y", "xl", "core")
PLANE = ("xh", "y", "xl")
BF16 = jnp.bfloat16
F32 = jnp.float32
TR, TC = 8, 64
CELLS = TR * TC
FEAT, CH, ZCH, GATES = 64, 128, 192, 512
TAPS = 3 * ZCH
GROUPS, SLOT = 8, 224
VMEM = 40 * 1024 * 1024


def to_neighbours(axes, last, first):
    count = lax.axis_size(axes)
    inner = [(i, i ^ 1) for i in range(count)]
    outer = [(i, i + 1 if i % 2 else i - 1) for i in range(1, count - 1)]
    even = lax.axis_index(axes[-1]) == 0
    near = lax.ppermute(jnp.where(even, last, first), axes, inner)
    far = lax.ppermute(jnp.where(even, first, last), axes, outer)
    return jnp.where(even, far, near), jnp.where(even, near, far)


def halo_rows(block):
    return to_neighbours(ROWS, block[TR - 1 :], block[:1])


def halo_cols(low, block, high):
    last = jnp.concatenate([low[:, TC - 1 :], block[:, TC - 1 :], high[:, TC - 1 :]], axis=0)
    first = jnp.concatenate([low[:, :1], block[:, :1], high[:, :1]], axis=0)
    return to_neighbours(COLS, last, first)


def shifted(row, before, after):
    place = lax.broadcasted_iota(jnp.int32, row.shape, 0)
    down = jnp.where(place == 0, before, pltpu.roll(row, 1, 0))
    up = jnp.where(place == TC - 1, after, pltpu.roll(row, TC - 1, 0))
    return down, up


def taps_kernel(stacked, taps):
    for r in range(TR):
        row = stacked[r].astype(F32)
        down, up = shifted(row, 0.0, 0.0)
        taps[(r + 1) * TC : (r + 2) * TC, :] = jnp.concatenate([down, row, up], axis=1).astype(BF16)


def half_products(taps, half_gates, half_bias, store, finish=lambda slot: None):
    for a in range(3):
        term = lax.dot_general(
            taps[a * TC : a * TC + CELLS, :],
            half_gates,
            (((0,), (0,)), ((), ())),
            preferred_element_type=F32,
        )
        begin = a * TAPS
        while begin < (a + 1) * TAPS:
            end = min((begin // SLOT + 1) * SLOT, (a + 1) * TAPS)
            group, top = begin // SLOT, begin % SLOT
            for j in range(2):
                block = term[begin - a * TAPS : end - a * TAPS, j * 128 : (j + 1) * 128]
                store(j * GROUPS + group, top, top + end - begin, block)
                if end % SLOT == 0:
                    finish(j * GROUPS + group)
            begin = end
    top = 3 * TAPS - (GROUPS - 1) * SLOT
    for j in range(2):
        slot = j * GROUPS + GROUPS - 1
        row = half_bias[:, j * 128 : (j + 1) * 128]
        store(slot, top, top + 16, jnp.concatenate([row, row], axis=0))
        store(slot, top + 16, SLOT, jnp.zeros((SLOT - top - 16, 128), F32))
        finish(slot)


def cell_kernel(
    own_taps, low, high, left, right, kernel, cell_prev, hidden_cot, cell_cot, bias,
    hidden_new, cell_new, grad_cell, grad_gates, taps, sums, send, gates,
):
    for r, halo in ((0, low), (TR + 1, high)):
        row = halo[0].astype(F32)
        down, up = shifted(row, left[r].astype(F32), right[r].astype(F32))
        taps[r * TC : (r + 1) * TC, :] = jnp.concatenate([down, row, up], axis=1).astype(BF16)
    place = lax.broadcasted_iota(jnp.int32, (16, ZCH), 0)
    for r in range(1, TR + 1):
        begin, end = r * TC, (r + 1) * TC
        taps[begin + 16 : end - 16, :] = own_taps[begin + 16 : end - 16, :]
        block = own_taps[begin : begin + 16, :].astype(F32)
        side = jnp.where(place == 0, left[r].astype(F32), block[:, :ZCH])
        taps[begin : begin + 16, :] = jnp.concatenate([side, block[:, ZCH:]], axis=1).astype(BF16)
        block = own_taps[end - 16 : end, :].astype(F32)
        side = jnp.where(place == 15, right[r].astype(F32), block[:, 2 * ZCH :])
        taps[end - 16 : end, :] = jnp.concatenate([block[:, : 2 * ZCH], side], axis=1).astype(BF16)
    total = jnp.dot(taps[0:CELLS, :], kernel[0], preferred_element_type=F32)
    total += jnp.dot(taps[TC : TC + CELLS, :], kernel[1], preferred_element_type=F32)
    total += jnp.dot(taps[2 * TC : 2 * TC + CELLS, :], kernel[2], preferred_element_type=F32)
    gates[...] = total + bias[...]
    bias_sum = jnp.zeros((8, GATES), F32)
    for r in range(TR):
        rows = slice(r * TC, (r + 1) * TC)
        in_gate = jax.nn.sigmoid(gates[rows, 0:CH])
        forget = jax.nn.sigmoid(gates[rows, CH : 2 * CH])
        out_gate = jax.nn.sigmoid(gates[rows, 2 * CH : 3 * CH])
        cand = jnp.tanh(gates[rows, 3 * CH :])
        before = cell_prev[r]
        new = forget * before + in_gate * cand
        squash = jnp.tanh(new)
        cell_new[r] = new
        hidden_new[r] = (out_gate * squash).astype(BF16)
        hid_cot = hidden_cot[r].astype(F32)
        total = cell_cot[r] + hid_cot * out_gate * (1.0 - squash * squash)
        grad_cell[r] = total * forget
        parts = [
            total * cand * in_gate * (1.0 - in_gate),
            total * before * forget * (1.0 - forget),
            hid_cot * squash * out_gate * (1.0 - out_gate),
            total * in_gate * (1.0 - cand * cand),
        ]
        rounded = jnp.concatenate([part.astype(BF16) for part in parts], axis=1)
        grad_gates[rows, :] = rounded
        wide = rounded.astype(F32).reshape(TC // 8, 8, GATES)
        bias_sum = bias_sum + jnp.sum(wide, axis=0)
    sums[...] = jnp.broadcast_to(jnp.sum(bias_sum, axis=0, keepdims=True), (8, GATES))
    columns = pl.ds(pl.multiple_of((1 - lax.axis_index("core")) * 256, 256), 256)

    def store(slot, top, end, block):
        send[slot, top:end, :] = block.astype(BF16)

    half_products(taps, grad_gates[:, columns], sums[:, columns], store)


def own_kernel(taps, grad_gates, sums, received, result, total, sent):
    columns = pl.ds(pl.multiple_of(lax.axis_index("core") * 256, 256), 256)

    def store(slot, top, end, block):
        total[slot, top:end, :] = (block + received[slot, top:end, :].astype(F32)).astype(BF16)

    def copy(slot):
        return pltpu.make_async_copy(total.at[slot], result.at[slot], sent.at[slot])

    half_products(
        taps, grad_gates[:, columns], sums[:, columns], store, lambda slot: copy(slot).start()
    )
    for slot in range(2 * GROUPS):
        copy(slot).wait()


def input_kernel(grad_gates, kernel, inner, edges, to_left, to_right, spread):
    spread[...] = jnp.zeros_like(spread)
    for a in range(3):
        spread[a * TC : a * TC + CELLS, :] += lax.dot_general(
            grad_gates[...], kernel[a], (((1,), (1,)), ((), ())), preferred_element_type=F32
        )
    lefts, rights = [], []
    for r in range(TR + 2):
        rows = spread[r * TC : (r + 1) * TC, :]
        lower, middle, upper = rows[:, :ZCH], rows[:, ZCH : 2 * ZCH], rows[:, 2 * ZCH :]
        _, from_lower = shifted(lower, 0.0, 0.0)
        from_upper, _ = shifted(upper, 0.0, 0.0)
        total = middle + from_lower + from_upper
        lefts.append(lower[:1])
        rights.append(upper[TC - 1 :])
        if r == 0:
            edges[0] = total
        elif r == TR + 1:
            edges[1] = total
        else:
            inner[(r - 1) * TC : r * TC, :] = total
    to_left[...] = jnp.concatenate(lefts, axis=0).astype(BF16)
    to_right[...] = jnp.concatenate(rights, axis=0).astype(BF16)


def with_columns(row, before, after):
    place = lax.broadcasted_iota(jnp.int32, row.shape, 0)
    return row + jnp.where(place == 0, before, 0.0) + jnp.where(place == TC - 1, after, 0.0)


def edge_kernel(edges, from_left, from_right, to_above, to_below):
    before, after = from_left[...].astype(F32), from_right[...].astype(F32)
    to_above[0] = with_columns(edges[0], before[:1], after[:1]).astype(BF16)
    to_below[0] = with_columns(edges[1], before[TR + 1 :], after[TR + 1 :]).astype(BF16)


def sum_kernel(
    inner, from_left, from_right, from_above, from_below, grad_features, grad_hidden
):
    before, after = from_left[...].astype(F32), from_right[...].astype(F32)
    for r in range(TR):
        row = inner[r * TC : (r + 1) * TC, :]
        row = with_columns(row, before[r + 1 : r + 2], after[r + 1 : r + 2])
        if r == 0:
            row = row + from_above[0].astype(F32)
        if r == TR - 1:
            row = row + from_below[0].astype(F32)
        grad_features[r] = row[:, :FEAT].astype(BF16)
        grad_hidden[r] = row[:, FEAT:].astype(BF16)


def place_half(slots, place, grad_kernel, grad_bias, last_slots, sems):
    last = 3 * TAPS - (GROUPS - 1) * SLOT
    copies = []
    for j in range(2):
        columns = pl.ds(pl.multiple_of(place * 256 + j * 128, 128), 128)
        slot = j * GROUPS + GROUPS - 1
        copies.append(
            pltpu.make_async_copy(
                slots.at[slot, last : last + 16, :], last_slots.at[j], sems.at[2 * GROUPS + j]
            )
        )
        for i in range(GROUPS):
            count = SLOT if i < GROUPS - 1 else last
            copies.append(
                pltpu.make_async_copy(
                    slots.at[j * GROUPS + i, 0:count, :],
                    grad_kernel.at[i * SLOT : i * SLOT + count, columns],
                    sems.at[j * GROUPS + i],
                )
            )
    for copy in copies:
        copy.start()
    for copy in copies:
        copy.wait()
    for j in range(2):
        columns = pl.ds(pl.multiple_of(place * 256 + j * 128, 128), 128)
        grad_bias[:, columns] = last_slots[j].astype(F32)[0:1]


def join_own_kernel(slots, grad_kernel, grad_bias, last_slots, sems):
    grad_bias[...] = jnp.zeros_like(grad_bias)
    place_half(slots, lax.axis_index("core"), grad_kernel, grad_bias, last_slots, sems)


def join_other_kernel(
    own_bias, slots, own_kernel_part, grad_kernel, grad_bias, last_slots, sems
):
    grad_bias[...] = own_bias[...]
    place_half(slots, 1 - lax.axis_index("core"), grad_kernel, grad_bias, last_slots, sems)


def call(body, outs, *args, scratch=(), flops=0, far=0, far_outs=0, aliases=()):
    moved = sum(x.size * x.dtype.itemsize for x in list(args) + list(outs))
    whole = pl.BlockSpec(memory_space=pltpu.VMEM)
    anywhere = pl.BlockSpec(memory_space=pl.ANY)
    return pl.pallas_call(
        body,
        out_shape=outs,
        in_specs=[whole] * (len(args) - far) + [anywhere] * far,
        out_specs=[anywhere] * far_outs + [whole] * (len(outs) - far_outs),
        input_output_aliases=dict(aliases),
        scratch_shapes=list(scratch),
        cost_estimate=pl.CostEstimate(flops=flops, bytes_accessed=moved, transcendentals=0),
        compiler_params=pltpu.CompilerParams(vmem_limit_bytes=VMEM),
    )(*args)


def copies_of(part, count):
    return lax.optimization_barrier(jnp.broadcast_to(part[None], (count,) + part.shape))


def local(features, hidden_prev, cell_prev, kernel, bias, hidden_cot, cell_cot):
    shape = jax.ShapeDtypeStruct
    work = 2 * CELLS * 3 * TAPS * GATES
    plane = lax.axis_size(PLANE)
    depth = lax.axis_size("z")
    swap = [(0, 1), (1, 0)]
    weights = kernel.reshape(3, TAPS, GATES)

    stacked = jnp.concatenate([features, hidden_prev], axis=2)
    low, high = halo_rows(stacked)
    (own_taps,) = call(
        taps_kernel, (shape(((TR + 2) * TC, TAPS), BF16),), stacked, flops=work
    )
    low, high, own_taps = lax.optimization_barrier((low, high, own_taps))
    left, right = halo_cols(low, stacked, high)
    hidden_new, cell_new, grad_cell, grad_gates, taps, sums, send = call(
        cell_kernel,
        (
            shape((TR, TC, CH), BF16),
            shape((TR, TC, CH), F32),
            shape((TR, TC, CH), F32),
            shape((CELLS, GATES), BF16),
            shape(((TR + 2) * TC, TAPS), BF16),
            shape((8, GATES), F32),
            shape((plane, SLOT, 128), BF16),
        ),
        own_taps, low, high, left, right, weights, cell_prev, hidden_cot, cell_cot,
        bias.reshape(1, GATES),
        scratch=[pltpu.VMEM((CELLS, GATES), F32)],
        flops=work + work // 2,
    )
    received = lax.ppermute(send, "core", swap)
    inner, edges, to_left, to_right = call(
        input_kernel,
        (
            shape((CELLS, ZCH), F32),
            shape((2, TC, ZCH), F32),
            shape((TR + 2, ZCH), BF16),
            shape((TR + 2, ZCH), BF16),
        ),
        grad_gates, weights,
        scratch=[pltpu.VMEM(((TR + 2) * TC, TAPS), F32)],
        flops=work,
    )
    received, to_left, to_right = lax.optimization_barrier((received, to_left, to_right))
    (half,) = call(
        own_kernel, (shape((plane, SLOT, 128), BF16),), taps, grad_gates, sums, received,
        scratch=[pltpu.VMEM((plane, SLOT, 128), BF16), pltpu.SemaphoreType.DMA((plane,))],
        flops=work // 2,
        far_outs=1,
    )
    half, to_left, to_right = lax.optimization_barrier((half, to_left, to_right))
    part = lax.all_to_all(half, PLANE, 0, 0, tiled=True)
    from_left, from_right = to_neighbours(COLS, to_right, to_left)
    part, from_left, from_right = lax.optimization_barrier((part, from_left, from_right))
    part = jnp.sum(part.astype(F32), axis=0).astype(BF16)
    part = lax.all_to_all(part.reshape(depth, SLOT // depth, 128), "z", 0, 0, tiled=True)
    scale = 1.0 / (TR * lax.axis_size(ROWS))
    part = (jnp.sum(part.astype(F32), axis=0) * scale).astype(BF16)
    part = lax.all_to_all(copies_of(part, depth), "z", 0, 0, tiled=True).reshape(SLOT, 128)
    copies, edges = lax.optimization_barrier((copies_of(part, plane), edges))
    half = lax.all_to_all(copies, PLANE, 0, 0, tiled=True)
    row = shape((1, TC, ZCH), BF16)
    to_above, to_below = call(edge_kernel, (row, row), edges, from_left, from_right)
    from_above, from_below = to_neighbours(ROWS, to_below, to_above)
    half, from_above, from_below = lax.optimization_barrier((half, from_above, from_below))
    grad_features, grad_hidden = call(
        sum_kernel,
        (shape((TR, TC, FEAT), BF16), shape((TR, TC, CH), BF16)),
        inner, from_left, from_right, from_above, from_below,
    )
    other = lax.ppermute(half, "core", swap)
    outs = (shape((3 * TAPS, GATES), BF16), shape((1, GATES), F32))
    scratch = [pltpu.VMEM((2, 16, 128), BF16), pltpu.SemaphoreType.DMA((2 * GROUPS + 2,))]
    grad_kernel, own_bias = call(
        join_own_kernel, outs, half, scratch=scratch, far=1, far_outs=1
    )
    other, grad_features, grad_hidden = lax.optimization_barrier(
        (other, grad_features, grad_hidden)
    )
    grad_kernel, grad_bias = call(
        join_other_kernel, outs, own_bias, other, grad_kernel,
        scratch=scratch, far=2, far_outs=1, aliases={2: 0},
    )
    return (
        hidden_new,
        cell_new,
        grad_features,
        grad_hidden,
        grad_cell,
        grad_kernel.reshape(3, 3, ZCH, GATES),
        grad_bias.reshape(GATES),
    )


def solution(mesh):
    grid = Mesh(mesh.devices.reshape(16, 2, 4, 2, 2), ROWS + COLS)
    tile = P(ROWS, COLS, None)
    return jax.shard_map(
        local,
        mesh=grid,
        in_specs=(tile, tile, tile, P(), P(), tile, tile),
        out_specs=(tile, tile, tile, tile, tile, P(), P()),
        check_vma=False,
    )
```

```python
import jax
import jax.numpy as jnp
from jax import lax
from jax.experimental import pallas as pl
from jax.experimental.pallas import tpu as pltpu
from jax.sharding import Mesh, PartitionSpec as P

ROWS = ("z", "xh")
COLS = ("y", "xl", "core")
PLANE = ("xh", "y", "xl")
BF16 = jnp.bfloat16
F32 = jnp.float32
TR, TC = 8, 64
CELLS = TR * TC
FEAT, CH, ZCH, GATES = 64, 128, 192, 512
TAPS = 3 * ZCH
GROUPS, SLOT = 8, 224
VMEM = 40 * 1024 * 1024


def to_neighbours(axes, last, first):
    count = lax.axis_size(axes)
    inner = [(i, i ^ 1) for i in range(count)]
    outer = [(i, i + 1 if i % 2 else i - 1) for i in range(1, count - 1)]
    even = lax.axis_index(axes[-1]) == 0
    near = lax.ppermute(jnp.where(even, last, first), axes, inner)
    far = lax.ppermute(jnp.where(even, first, last), axes, outer)
    return jnp.where(even, far, near), jnp.where(even, near, far)


def halo_rows(block):
    return to_neighbours(ROWS, block[TR - 1 :], block[:1])


def halo_cols(low, block, high):
    last = jnp.concatenate([low[:, TC - 1 :], block[:, TC - 1 :], high[:, TC - 1 :]], axis=0)
    first = jnp.concatenate([low[:, :1], block[:, :1], high[:, :1]], axis=0)
    return to_neighbours(COLS, last, first)


def shifted(row, before, after):
    place = lax.broadcasted_iota(jnp.int32, row.shape, 0)
    down = jnp.where(place == 0, before, pltpu.roll(row, 1, 0))
    up = jnp.where(place == TC - 1, after, pltpu.roll(row, TC - 1, 0))
    return down, up


def taps_kernel(stacked, taps):
    for r in range(TR):
        row = stacked[r].astype(F32)
        down, up = shifted(row, 0.0, 0.0)
        taps[(r + 1) * TC : (r + 2) * TC, :] = jnp.concatenate([down, row, up], axis=1).astype(BF16)


def half_products(taps, half_gates, half_bias, store, finish=lambda slot: None):
    for a in range(3):
        term = lax.dot_general(
            taps[a * TC : a * TC + CELLS, :],
            half_gates,
            (((0,), (0,)), ((), ())),
            preferred_element_type=F32,
        )
        begin = a * TAPS
        while begin < (a + 1) * TAPS:
            end = min((begin // SLOT + 1) * SLOT, (a + 1) * TAPS)
            group, top = begin // SLOT, begin % SLOT
            for j in range(2):
                block = term[begin - a * TAPS : end - a * TAPS, j * 128 : (j + 1) * 128]
                store(j * GROUPS + group, top, top + end - begin, block)
                if end % SLOT == 0:
                    finish(j * GROUPS + group)
            begin = end
    top = 3 * TAPS - (GROUPS - 1) * SLOT
    for j in range(2):
        slot = j * GROUPS + GROUPS - 1
        row = half_bias[:, j * 128 : (j + 1) * 128]
        store(slot, top, top + 16, jnp.concatenate([row, row], axis=0))
        store(slot, top + 16, SLOT, jnp.zeros((SLOT - top - 16, 128), F32))
        finish(slot)


def cell_kernel(
    own_taps, low, high, left, right, kernel, cell_prev, hidden_cot, cell_cot, bias,
    hidden_out, cell_out, grad_cell_out, grad_gates, taps, sums, send,
    gates, hidden_new, cell_new, grad_cell, sent,
):
    for r, halo in ((0, low), (TR + 1, high)):
        row = halo[0].astype(F32)
        down, up = shifted(row, left[r].astype(F32), right[r].astype(F32))
        taps[r * TC : (r + 1) * TC, :] = jnp.concatenate([down, row, up], axis=1).astype(BF16)
    place = lax.broadcasted_iota(jnp.int32, (16, ZCH), 0)
    for r in range(1, TR + 1):
        begin, end = r * TC, (r + 1) * TC
        taps[begin + 16 : end - 16, :] = own_taps[begin + 16 : end - 16, :]
        block = own_taps[begin : begin + 16, :].astype(F32)
        side = jnp.where(place == 0, left[r].astype(F32), block[:, :ZCH])
        taps[begin : begin + 16, :] = jnp.concatenate([side, block[:, ZCH:]], axis=1).astype(BF16)
        block = own_taps[end - 16 : end, :].astype(F32)
        side = jnp.where(place == 15, right[r].astype(F32), block[:, 2 * ZCH :])
        taps[end - 16 : end, :] = jnp.concatenate([block[:, : 2 * ZCH], side], axis=1).astype(BF16)
    total = jnp.dot(taps[0:CELLS, :], kernel[0], preferred_element_type=F32)
    total += jnp.dot(taps[TC : TC + CELLS, :], kernel[1], preferred_element_type=F32)
    total += jnp.dot(taps[2 * TC : 2 * TC + CELLS, :], kernel[2], preferred_element_type=F32)
    gates[...] = total + bias[...]
    bias_sum = jnp.zeros((8, GATES), F32)
    for r in range(TR):
        rows = slice(r * TC, (r + 1) * TC)
        in_gate = jax.nn.sigmoid(gates[rows, 0:CH])
        forget = jax.nn.sigmoid(gates[rows, CH : 2 * CH])
        out_gate = jax.nn.sigmoid(gates[rows, 2 * CH : 3 * CH])
        cand = jnp.tanh(gates[rows, 3 * CH :])
        before = cell_prev[r]
        new = forget * before + in_gate * cand
        squash = jnp.tanh(new)
        cell_new[r] = new
        hidden_new[r] = (out_gate * squash).astype(BF16)
        hid_cot = hidden_cot[r].astype(F32)
        total = cell_cot[r] + hid_cot * out_gate * (1.0 - squash * squash)
        grad_cell[r] = total * forget
        parts = [
            total * cand * in_gate * (1.0 - in_gate),
            total * before * forget * (1.0 - forget),
            hid_cot * squash * out_gate * (1.0 - out_gate),
            total * in_gate * (1.0 - cand * cand),
        ]
        rounded = jnp.concatenate([part.astype(BF16) for part in parts], axis=1)
        grad_gates[rows, :] = rounded
        wide = rounded.astype(F32).reshape(TC // 8, 8, GATES)
        bias_sum = bias_sum + jnp.sum(wide, axis=0)
    copies = [
        pltpu.make_async_copy(source, target, sent.at[i])
        for i, (source, target) in enumerate(
            ((hidden_new, hidden_out), (cell_new, cell_out), (grad_cell, grad_cell_out))
        )
    ]
    for copy in copies:
        copy.start()
    sums[...] = jnp.broadcast_to(jnp.sum(bias_sum, axis=0, keepdims=True), (8, GATES))
    columns = pl.ds(pl.multiple_of((1 - lax.axis_index("core")) * 256, 256), 256)

    def store(slot, top, end, block):
        send[slot, top:end, :] = block.astype(BF16)

    half_products(taps, grad_gates[:, columns], sums[:, columns], store)
    for copy in copies:
        copy.wait()


def own_kernel(taps, grad_gates, sums, received, result, total, sent):
    columns = pl.ds(pl.multiple_of(lax.axis_index("core") * 256, 256), 256)

    def store(slot, top, end, block):
        total[slot, top:end, :] = (block + received[slot, top:end, :].astype(F32)).astype(BF16)

    def copy(slot):
        return pltpu.make_async_copy(total.at[slot], result.at[slot], sent.at[slot])

    half_products(
        taps, grad_gates[:, columns], sums[:, columns], store, lambda slot: copy(slot).start()
    )
    for slot in range(2 * GROUPS):
        copy(slot).wait()


def input_kernel(grad_gates, kernel, inner, to_above, to_below, lefts, rights, spread):
    spread[...] = jnp.zeros_like(spread)
    for a in range(3):
        spread[a * TC : a * TC + CELLS, :] += lax.dot_general(
            grad_gates[...], kernel[a], (((1,), (1,)), ((), ())), preferred_element_type=F32
        )
    sides = []
    for r in range(TR + 2):
        rows = spread[r * TC : (r + 1) * TC, :]
        lower, middle, upper = rows[:, :ZCH], rows[:, ZCH : 2 * ZCH], rows[:, 2 * ZCH :]
        _, from_lower = shifted(lower, 0.0, 0.0)
        from_upper, _ = shifted(upper, 0.0, 0.0)
        total = middle + from_lower + from_upper
        if 0 < r < TR + 1:
            inner[(r - 1) * TC : r * TC, :] = total
            sides.append((lower[:1], upper[TC - 1 :]))
        else:
            target = to_above if r == 0 else to_below
            corners = [lower[:1], upper[TC - 1 :], jnp.zeros((14, ZCH), F32)]
            target[0:TC, :] = total.astype(BF16)
            target[TC : TC + 16, :] = jnp.concatenate(corners, axis=0).astype(BF16)
    lefts[...] = jnp.concatenate([left for left, _ in sides], axis=0)
    rights[...] = jnp.concatenate([right for _, right in sides], axis=0)


def side_kernel(lefts, rights, from_above, from_below, to_left, to_right):
    place = lax.broadcasted_iota(jnp.int32, (TR, ZCH), 0)
    above = from_above[TC : TC + 16, :].astype(F32)
    below = from_below[TC : TC + 16, :].astype(F32)
    for i, own, target in ((0, lefts, to_left), (1, rights, to_right)):
        extra = jnp.where(place == 0, above[i : i + 1], 0.0)
        extra += jnp.where(place == TR - 1, below[i : i + 1], 0.0)
        target[...] = (own[...] + extra).astype(BF16)


def sum_kernel(
    inner, from_above, from_below, from_left, from_right, grad_features, grad_hidden
):
    before, after = from_left[...].astype(F32), from_right[...].astype(F32)
    place = lax.broadcasted_iota(jnp.int32, (TC, ZCH), 0)
    for r in range(TR):
        row = inner[r * TC : (r + 1) * TC, :]
        row += jnp.where(place == 0, before[r : r + 1], 0.0)
        row += jnp.where(place == TC - 1, after[r : r + 1], 0.0)
        if r == 0:
            row += from_above[0:TC, :].astype(F32)
        if r == TR - 1:
            row += from_below[0:TC, :].astype(F32)
        grad_features[r] = row[:, :FEAT].astype(BF16)
        grad_hidden[r] = row[:, FEAT:].astype(BF16)


def plane_sum_kernel(parts, total):
    result = parts[0].astype(F32)
    for i in range(1, parts.shape[0]):
        result += parts[i].astype(F32)
    total[...] = result.astype(BF16)


def copies_kernel(part, copies, sems):
    moves = [
        pltpu.make_async_copy(part, copies.at[i], sems.at[i]) for i in range(copies.shape[0])
    ]
    for move in moves:
        move.start()
    for move in moves:
        move.wait()


def place_half(slots, place, grad_kernel, last_slots, sems):
    last = 3 * TAPS - (GROUPS - 1) * SLOT
    heads, copies = [], []
    for j in range(2):
        columns = pl.ds(pl.multiple_of(place * 256 + j * 128, 128), 128)
        slot = j * GROUPS + GROUPS - 1
        heads.append(
            pltpu.make_async_copy(
                slots.at[slot, last : last + 16, :], last_slots.at[j], sems.at[2 * GROUPS + j]
            )
        )
        for i in range(GROUPS):
            count = SLOT if i < GROUPS - 1 else last
            copies.append(
                pltpu.make_async_copy(
                    slots.at[j * GROUPS + i, 0:count, :],
                    grad_kernel.at[i * SLOT : i * SLOT + count, columns],
                    sems.at[j * GROUPS + i],
                )
            )
    for copy in heads + copies:
        copy.start()
    for copy in heads:
        copy.wait()
    return [last_slots[j].astype(F32)[0:1] for j in range(2)], copies


def join_own_kernel(slots, grad_kernel, own_bias, last_slots, sems):
    core = lax.axis_index("core")
    rows, copies = place_half(slots, core, grad_kernel, last_slots, sems)
    own_bias[...] = jnp.zeros_like(own_bias)
    for j in range(2):
        own_bias[:, pl.ds(pl.multiple_of(core * 256 + j * 128, 128), 128)] = rows[j]
    for copy in copies:
        copy.wait()


def join_other_kernel(
    own_bias, slots, own_kernel_part, grad_kernel, grad_bias, last_slots, bias, sems
):
    place = 1 - lax.axis_index("core")
    rows, copies = place_half(slots, place, grad_kernel, last_slots, sems)
    bias[...] = own_bias[...]
    for j in range(2):
        bias[:, pl.ds(pl.multiple_of(place * 256 + j * 128, 128), 128)] = rows[j]
    copies.append(pltpu.make_async_copy(bias, grad_bias, sems.at[2 * GROUPS + 2]))
    copies[-1].start()
    for copy in copies:
        copy.wait()


def call(body, outs, *args, scratch=(), flops=0, far=0, far_outs=0, aliases=()):
    moved = sum(x.size * x.dtype.itemsize for x in list(args) + list(outs))
    whole = pl.BlockSpec(memory_space=pltpu.VMEM)
    anywhere = pl.BlockSpec(memory_space=pl.ANY)
    return pl.pallas_call(
        body,
        out_shape=outs,
        in_specs=[whole] * (len(args) - far) + [anywhere] * far,
        out_specs=[anywhere] * far_outs + [whole] * (len(outs) - far_outs),
        input_output_aliases=dict(aliases),
        scratch_shapes=list(scratch),
        cost_estimate=pl.CostEstimate(flops=flops, bytes_accessed=moved, transcendentals=0),
        compiler_params=pltpu.CompilerParams(vmem_limit_bytes=VMEM),
    )(*args)


def copies_of(part, count):
    return lax.optimization_barrier(jnp.broadcast_to(part[None], (count,) + part.shape))


def local(features, hidden_prev, cell_prev, kernel, bias, hidden_cot, cell_cot):
    shape = jax.ShapeDtypeStruct
    work = 2 * CELLS * 3 * TAPS * GATES
    plane = lax.axis_size(PLANE)
    depth = lax.axis_size("z")
    swap = [(0, 1), (1, 0)]
    weights = kernel.reshape(3, TAPS, GATES)

    stacked = jnp.concatenate([features, hidden_prev], axis=2)
    low, high = halo_rows(stacked)
    (own_taps,) = call(
        taps_kernel, (shape(((TR + 2) * TC, TAPS), BF16),), stacked, flops=work
    )
    low, high, own_taps = lax.optimization_barrier((low, high, own_taps))
    left, right = halo_cols(low, stacked, high)
    hidden_new, cell_new, grad_cell, grad_gates, taps, sums, send = call(
        cell_kernel,
        (
            shape((TR, TC, CH), BF16),
            shape((TR, TC, CH), F32),
            shape((TR, TC, CH), F32),
            shape((CELLS, GATES), BF16),
            shape(((TR + 2) * TC, TAPS), BF16),
            shape((8, GATES), F32),
            shape((plane, SLOT, 128), BF16),
        ),
        own_taps, low, high, left, right, weights, cell_prev, hidden_cot, cell_cot,
        bias.reshape(1, GATES),
        scratch=[
            pltpu.VMEM((CELLS, GATES), F32),
            pltpu.VMEM((TR, TC, CH), BF16),
            pltpu.VMEM((TR, TC, CH), F32),
            pltpu.VMEM((TR, TC, CH), F32),
            pltpu.SemaphoreType.DMA((3,)),
        ],
        flops=work + work // 2,
        far_outs=3,
    )
    received = lax.ppermute(send, "core", swap)
    inner, to_above, to_below, lefts, rights = call(
        input_kernel,
        (
            shape((CELLS, ZCH), F32),
            shape((TC + 16, ZCH), BF16),
            shape((TC + 16, ZCH), BF16),
            shape((TR, ZCH), F32),
            shape((TR, ZCH), F32),
        ),
        grad_gates, weights,
        scratch=[pltpu.VMEM(((TR + 2) * TC, TAPS), F32)],
        flops=work,
    )
    received, to_above, to_below = lax.optimization_barrier((received, to_above, to_below))
    (half,) = call(
        own_kernel, (shape((plane, SLOT, 128), BF16),), taps, grad_gates, sums, received,
        scratch=[pltpu.VMEM((plane, SLOT, 128), BF16), pltpu.SemaphoreType.DMA((plane,))],
        flops=work // 2,
        far_outs=1,
    )
    half, to_above, to_below = lax.optimization_barrier((half, to_above, to_below))
    part = lax.all_to_all(half, PLANE, 0, 0, tiled=True)
    from_above, from_below = to_neighbours(ROWS, to_below, to_above)
    part, from_above, from_below = lax.optimization_barrier((part, from_above, from_below))
    (part,) = call(plane_sum_kernel, (shape((SLOT, 128), BF16),), part)
    part = lax.all_to_all(part.reshape(depth, SLOT // depth, 128), "z", 0, 0, tiled=True)
    scale = 1.0 / (TR * lax.axis_size(ROWS))
    part = (jnp.sum(part.astype(F32), axis=0) * scale).astype(BF16)
    part = lax.all_to_all(copies_of(part, depth), "z", 0, 0, tiled=True).reshape(SLOT, 128)
    (copies,) = call(
        copies_kernel, (shape((plane, SLOT, 128), BF16),), part,
        scratch=[pltpu.SemaphoreType.DMA((plane,))],
        far_outs=1,
    )
    copies, lefts = lax.optimization_barrier((copies, lefts))
    half = lax.all_to_all(copies, PLANE, 0, 0, tiled=True)
    side = shape((TR, ZCH), BF16)
    to_left, to_right = call(side_kernel, (side, side), lefts, rights, from_above, from_below)
    from_left, from_right = to_neighbours(COLS, to_right, to_left)
    half, from_left, from_right = lax.optimization_barrier((half, from_left, from_right))
    grad_features, grad_hidden = call(
        sum_kernel,
        (shape((TR, TC, FEAT), BF16), shape((TR, TC, CH), BF16)),
        inner, from_above, from_below, from_left, from_right,
    )
    other = lax.ppermute(half, "core", swap)
    outs = (shape((3 * TAPS, GATES), BF16), shape((1, GATES), F32))
    tails = pltpu.VMEM((2, 16, 128), BF16)
    sems = pltpu.SemaphoreType.DMA((2 * GROUPS + 3,))
    grad_kernel, own_bias = call(
        join_own_kernel, outs, half, scratch=[tails, sems], far=1, far_outs=1
    )
    other, grad_features, grad_hidden = lax.optimization_barrier(
        (other, grad_features, grad_hidden)
    )
    grad_kernel, grad_bias = call(
        join_other_kernel, outs, own_bias, other, grad_kernel,
        scratch=[tails, pltpu.VMEM((1, GATES), F32), sems],
        far=2, far_outs=2, aliases={2: 0},
    )
    return (
        hidden_new,
        cell_new,
        grad_features,
        grad_hidden,
        grad_cell,
        grad_kernel.reshape(3, 3, ZCH, GATES),
        grad_bias.reshape(GATES),
    )


def solution(mesh):
    grid = Mesh(mesh.devices.reshape(16, 2, 4, 2, 2), ROWS + COLS)
    tile = P(ROWS, COLS, None)
    return jax.shard_map(
        local,
        mesh=grid,
        in_specs=(tile, tile, tile, P(), P(), tile, tile),
        out_specs=(tile, tile, tile, tile, tile, P(), P()),
        check_vma=False,
    )
```

```python
import jax
import jax.numpy as jnp
from jax import lax
from jax.experimental import pallas as pl
from jax.experimental.pallas import tpu as pltpu
from jax.sharding import Mesh, PartitionSpec as P

ROWS = ("z", "xh")
COLS = ("y", "xl", "core")
PLANE = ("xh", "y", "xl")
BF16 = jnp.bfloat16
F32 = jnp.float32
TR, TC = 8, 64
CELLS = TR * TC
FEAT, CH, ZCH, GATES = 64, 128, 192, 512
TAPS = 3 * ZCH
GROUPS, SLOT = 8, 224
VMEM = 40 * 1024 * 1024


def to_neighbours(axes, last, first):
    count = lax.axis_size(axes)
    inner = [(i, i ^ 1) for i in range(count)]
    outer = [(i, i + 1 if i % 2 else i - 1) for i in range(1, count - 1)]
    even = lax.axis_index(axes[-1]) == 0
    near = lax.ppermute(jnp.where(even, last, first), axes, inner)
    far = lax.ppermute(jnp.where(even, first, last), axes, outer)
    return jnp.where(even, far, near), jnp.where(even, near, far)


def halo_rows(block):
    return to_neighbours(ROWS, block[TR - 1 :], block[:1])


def halo_cols(low, block, high):
    last = jnp.concatenate([low[:, TC - 1 :], block[:, TC - 1 :], high[:, TC - 1 :]], axis=0)
    first = jnp.concatenate([low[:, :1], block[:, :1], high[:, :1]], axis=0)
    return to_neighbours(COLS, last, first)


def shifted(row, before, after):
    place = lax.broadcasted_iota(jnp.int32, row.shape, 0)
    down = jnp.where(place == 0, before, pltpu.roll(row, 1, 0))
    up = jnp.where(place == TC - 1, after, pltpu.roll(row, TC - 1, 0))
    return down, up


def taps_kernel(stacked, taps):
    for r in range(TR):
        row = stacked[r].astype(F32)
        down, up = shifted(row, 0.0, 0.0)
        taps[(r + 1) * TC : (r + 2) * TC, :] = jnp.concatenate([down, row, up], axis=1).astype(BF16)


def half_products(taps, half_gates, half_bias, store, finish=lambda slot: None):
    for a in range(3):
        term = lax.dot_general(
            taps[a * TC : a * TC + CELLS, :],
            half_gates,
            (((0,), (0,)), ((), ())),
            preferred_element_type=F32,
        )
        begin = a * TAPS
        while begin < (a + 1) * TAPS:
            end = min((begin // SLOT + 1) * SLOT, (a + 1) * TAPS)
            group, top = begin // SLOT, begin % SLOT
            for j in range(2):
                block = term[begin - a * TAPS : end - a * TAPS, j * 128 : (j + 1) * 128]
                store(j * GROUPS + group, top, top + end - begin, block)
                if end % SLOT == 0:
                    finish(j * GROUPS + group)
            begin = end
    top = 3 * TAPS - (GROUPS - 1) * SLOT
    for j in range(2):
        slot = j * GROUPS + GROUPS - 1
        row = half_bias[:, j * 128 : (j + 1) * 128]
        store(slot, top, top + 16, jnp.concatenate([row, row], axis=0))
        store(slot, top + 16, SLOT, jnp.zeros((SLOT - top - 16, 128), F32))
        finish(slot)


def cell_kernel(
    own_taps, low, high, left, right, kernel, cell_prev, hidden_cot, cell_cot, bias,
    hidden_out, cell_out, grad_cell_out, grad_gates, taps, sums, send,
    gates, hidden_new, cell_new, grad_cell, sent,
):
    for r, halo in ((0, low), (TR + 1, high)):
        row = halo[0].astype(F32)
        down, up = shifted(row, left[r].astype(F32), right[r].astype(F32))
        taps[r * TC : (r + 1) * TC, :] = jnp.concatenate([down, row, up], axis=1).astype(BF16)
    place = lax.broadcasted_iota(jnp.int32, (16, ZCH), 0)
    for r in range(1, TR + 1):
        begin, end = r * TC, (r + 1) * TC
        taps[begin + 16 : end - 16, :] = own_taps[begin + 16 : end - 16, :]
        block = own_taps[begin : begin + 16, :].astype(F32)
        side = jnp.where(place == 0, left[r].astype(F32), block[:, :ZCH])
        taps[begin : begin + 16, :] = jnp.concatenate([side, block[:, ZCH:]], axis=1).astype(BF16)
        block = own_taps[end - 16 : end, :].astype(F32)
        side = jnp.where(place == 15, right[r].astype(F32), block[:, 2 * ZCH :])
        taps[end - 16 : end, :] = jnp.concatenate([block[:, : 2 * ZCH], side], axis=1).astype(BF16)
    wide = jnp.concatenate([taps[a * TC : a * TC + CELLS, :] for a in range(3)], axis=1)
    weights = kernel[...].reshape(3 * TAPS, GATES)
    total = jnp.dot(wide, weights, preferred_element_type=F32)
    gates[...] = total + bias[...]
    bias_sum = jnp.zeros((8, GATES), F32)
    for r in range(TR):
        rows = slice(r * TC, (r + 1) * TC)
        in_gate = jax.nn.sigmoid(gates[rows, 0:CH])
        forget = jax.nn.sigmoid(gates[rows, CH : 2 * CH])
        out_gate = jax.nn.sigmoid(gates[rows, 2 * CH : 3 * CH])
        cand = jnp.tanh(gates[rows, 3 * CH :])
        before = cell_prev[r]
        new = forget * before + in_gate * cand
        squash = jnp.tanh(new)
        cell_new[r] = new
        hidden_new[r] = (out_gate * squash).astype(BF16)
        hid_cot = hidden_cot[r].astype(F32)
        total = cell_cot[r] + hid_cot * out_gate * (1.0 - squash * squash)
        grad_cell[r] = total * forget
        parts = [
            total * cand * in_gate * (1.0 - in_gate),
            total * before * forget * (1.0 - forget),
            hid_cot * squash * out_gate * (1.0 - out_gate),
            total * in_gate * (1.0 - cand * cand),
        ]
        rounded = jnp.concatenate([part.astype(BF16) for part in parts], axis=1)
        grad_gates[rows, :] = rounded
        wide = rounded.astype(F32).reshape(TC // 8, 8, GATES)
        bias_sum = bias_sum + jnp.sum(wide, axis=0)
    copies = [
        pltpu.make_async_copy(source, target, sent.at[i])
        for i, (source, target) in enumerate(
            ((hidden_new, hidden_out), (cell_new, cell_out), (grad_cell, grad_cell_out))
        )
    ]
    for copy in copies:
        copy.start()
    sums[...] = jnp.broadcast_to(jnp.sum(bias_sum, axis=0, keepdims=True), (8, GATES))
    columns = pl.ds(pl.multiple_of((1 - lax.axis_index("core")) * 256, 256), 256)

    def store(slot, top, end, block):
        send[slot, top:end, :] = block.astype(BF16)

    half_products(taps, grad_gates[:, columns], sums[:, columns], store)
    for copy in copies:
        copy.wait()


def own_kernel(taps, grad_gates, sums, received, result, total, sent):
    columns = pl.ds(pl.multiple_of(lax.axis_index("core") * 256, 256), 256)

    def store(slot, top, end, block):
        total[slot, top:end, :] = (block + received[slot, top:end, :].astype(F32)).astype(BF16)

    def copy(slot):
        return pltpu.make_async_copy(total.at[slot], result.at[slot], sent.at[slot])

    half_products(
        taps, grad_gates[:, columns], sums[:, columns], store, lambda slot: copy(slot).start()
    )
    for slot in range(2 * GROUPS):
        copy(slot).wait()


def input_kernel(grad_gates, kernel, inner, to_above, to_below, lefts, rights, spread):
    spread[...] = jnp.zeros_like(spread)
    for a in range(3):
        spread[a * TC : a * TC + CELLS, :] += lax.dot_general(
            grad_gates[...], kernel[a], (((1,), (1,)), ((), ())), preferred_element_type=F32
        )
    sides = []
    for r in range(TR + 2):
        rows = spread[r * TC : (r + 1) * TC, :]
        lower, middle, upper = rows[:, :ZCH], rows[:, ZCH : 2 * ZCH], rows[:, 2 * ZCH :]
        _, from_lower = shifted(lower, 0.0, 0.0)
        from_upper, _ = shifted(upper, 0.0, 0.0)
        total = middle + from_lower + from_upper
        if 0 < r < TR + 1:
            inner[(r - 1) * TC : r * TC, :] = total
            sides.append((lower[:1], upper[TC - 1 :]))
        else:
            target = to_above if r == 0 else to_below
            corners = [lower[:1], upper[TC - 1 :], jnp.zeros((14, ZCH), F32)]
            target[0:TC, :] = total.astype(BF16)
            target[TC : TC + 16, :] = jnp.concatenate(corners, axis=0).astype(BF16)
    lefts[...] = jnp.concatenate([left for left, _ in sides], axis=0)
    rights[...] = jnp.concatenate([right for _, right in sides], axis=0)


def side_kernel(lefts, rights, from_above, from_below, to_left, to_right):
    place = lax.broadcasted_iota(jnp.int32, (TR, ZCH), 0)
    above = from_above[TC : TC + 16, :].astype(F32)
    below = from_below[TC : TC + 16, :].astype(F32)
    for i, own, target in ((0, lefts, to_left), (1, rights, to_right)):
        extra = jnp.where(place == 0, above[i : i + 1], 0.0)
        extra += jnp.where(place == TR - 1, below[i : i + 1], 0.0)
        target[...] = (own[...] + extra).astype(BF16)


def sum_kernel(
    inner, from_above, from_below, from_left, from_right, grad_features, grad_hidden
):
    before, after = from_left[...].astype(F32), from_right[...].astype(F32)
    place = lax.broadcasted_iota(jnp.int32, (TC, ZCH), 0)
    for r in range(TR):
        row = inner[r * TC : (r + 1) * TC, :]
        row += jnp.where(place == 0, before[r : r + 1], 0.0)
        row += jnp.where(place == TC - 1, after[r : r + 1], 0.0)
        if r == 0:
            row += from_above[0:TC, :].astype(F32)
        if r == TR - 1:
            row += from_below[0:TC, :].astype(F32)
        grad_features[r] = row[:, :FEAT].astype(BF16)
        grad_hidden[r] = row[:, FEAT:].astype(BF16)


def plane_sum_kernel(parts, total):
    result = parts[0].astype(F32)
    for i in range(1, parts.shape[0]):
        result += parts[i].astype(F32)
    total[...] = result.astype(BF16)


def copies_kernel(part, copies, sems):
    moves = [
        pltpu.make_async_copy(part, copies.at[i], sems.at[i]) for i in range(copies.shape[0])
    ]
    for move in moves:
        move.start()
    for move in moves:
        move.wait()


def place_half(slots, place, grad_kernel, last_slots, sems):
    last = 3 * TAPS - (GROUPS - 1) * SLOT
    heads, copies = [], []
    for j in range(2):
        columns = pl.ds(pl.multiple_of(place * 256 + j * 128, 128), 128)
        slot = j * GROUPS + GROUPS - 1
        heads.append(
            pltpu.make_async_copy(
                slots.at[slot, last : last + 16, :], last_slots.at[j], sems.at[2 * GROUPS + j]
            )
        )
        for i in range(GROUPS):
            count = SLOT if i < GROUPS - 1 else last
            copies.append(
                pltpu.make_async_copy(
                    slots.at[j * GROUPS + i, 0:count, :],
                    grad_kernel.at[i * SLOT : i * SLOT + count, columns],
                    sems.at[j * GROUPS + i],
                )
            )
    for copy in heads + copies:
        copy.start()
    for copy in heads:
        copy.wait()
    return [last_slots[j].astype(F32)[0:1] for j in range(2)], copies


def join_own_kernel(slots, grad_kernel, own_bias, last_slots, sems):
    core = lax.axis_index("core")
    rows, copies = place_half(slots, core, grad_kernel, last_slots, sems)
    own_bias[...] = jnp.zeros_like(own_bias)
    for j in range(2):
        own_bias[:, pl.ds(pl.multiple_of(core * 256 + j * 128, 128), 128)] = rows[j]
    for copy in copies:
        copy.wait()


def join_other_kernel(
    own_bias, slots, own_kernel_part, grad_kernel, grad_bias, last_slots, bias, sems
):
    place = 1 - lax.axis_index("core")
    rows, copies = place_half(slots, place, grad_kernel, last_slots, sems)
    bias[...] = own_bias[...]
    for j in range(2):
        bias[:, pl.ds(pl.multiple_of(place * 256 + j * 128, 128), 128)] = rows[j]
    copies.append(pltpu.make_async_copy(bias, grad_bias, sems.at[2 * GROUPS + 2]))
    copies[-1].start()
    for copy in copies:
        copy.wait()


def call(body, outs, *args, scratch=(), flops=0, far=0, far_outs=0, aliases=()):
    moved = sum(x.size * x.dtype.itemsize for x in list(args) + list(outs))
    whole = pl.BlockSpec(memory_space=pltpu.VMEM)
    anywhere = pl.BlockSpec(memory_space=pl.ANY)
    return pl.pallas_call(
        body,
        out_shape=outs,
        in_specs=[whole] * (len(args) - far) + [anywhere] * far,
        out_specs=[anywhere] * far_outs + [whole] * (len(outs) - far_outs),
        input_output_aliases=dict(aliases),
        scratch_shapes=list(scratch),
        cost_estimate=pl.CostEstimate(flops=flops, bytes_accessed=moved, transcendentals=0),
        compiler_params=pltpu.CompilerParams(vmem_limit_bytes=VMEM),
    )(*args)


def copies_of(part, count):
    return lax.optimization_barrier(jnp.broadcast_to(part[None], (count,) + part.shape))


def local(features, hidden_prev, cell_prev, kernel, bias, hidden_cot, cell_cot):
    shape = jax.ShapeDtypeStruct
    work = 2 * CELLS * 3 * TAPS * GATES
    plane = lax.axis_size(PLANE)
    depth = lax.axis_size("z")
    swap = [(0, 1), (1, 0)]
    weights = kernel.reshape(3, TAPS, GATES)

    stacked = jnp.concatenate([features, hidden_prev], axis=2)
    low, high = halo_rows(stacked)
    (own_taps,) = call(
        taps_kernel, (shape(((TR + 2) * TC, TAPS), BF16),), stacked, flops=work
    )
    low, high, own_taps = lax.optimization_barrier((low, high, own_taps))
    left, right = halo_cols(low, stacked, high)
    hidden_new, cell_new, grad_cell, grad_gates, taps, sums, send = call(
        cell_kernel,
        (
            shape((TR, TC, CH), BF16),
            shape((TR, TC, CH), F32),
            shape((TR, TC, CH), F32),
            shape((CELLS, GATES), BF16),
            shape(((TR + 2) * TC, TAPS), BF16),
            shape((8, GATES), F32),
            shape((plane, SLOT, 128), BF16),
        ),
        own_taps, low, high, left, right, weights, cell_prev, hidden_cot, cell_cot,
        bias.reshape(1, GATES),
        scratch=[
            pltpu.VMEM((CELLS, GATES), F32),
            pltpu.VMEM((TR, TC, CH), BF16),
            pltpu.VMEM((TR, TC, CH), F32),
            pltpu.VMEM((TR, TC, CH), F32),
            pltpu.SemaphoreType.DMA((3,)),
        ],
        flops=work + work // 2,
        far_outs=3,
    )
    received = lax.ppermute(send, "core", swap)
    inner, to_above, to_below, lefts, rights = call(
        input_kernel,
        (
            shape((CELLS, ZCH), F32),
            shape((TC + 16, ZCH), BF16),
            shape((TC + 16, ZCH), BF16),
            shape((TR, ZCH), F32),
            shape((TR, ZCH), F32),
        ),
        grad_gates, weights,
        scratch=[pltpu.VMEM(((TR + 2) * TC, TAPS), F32)],
        flops=work,
    )
    received, to_above, to_below = lax.optimization_barrier((received, to_above, to_below))
    (half,) = call(
        own_kernel, (shape((plane, SLOT, 128), BF16),), taps, grad_gates, sums, received,
        scratch=[pltpu.VMEM((plane, SLOT, 128), BF16), pltpu.SemaphoreType.DMA((plane,))],
        flops=work // 2,
        far_outs=1,
    )
    half, to_above, to_below = lax.optimization_barrier((half, to_above, to_below))
    part = lax.all_to_all(half, PLANE, 0, 0, tiled=True)
    from_above, from_below = to_neighbours(ROWS, to_below, to_above)
    part, from_above, from_below = lax.optimization_barrier((part, from_above, from_below))
    (part,) = call(plane_sum_kernel, (shape((SLOT, 128), BF16),), part)
    part = lax.all_to_all(part.reshape(depth, SLOT // depth, 128), "z", 0, 0, tiled=True)
    scale = 1.0 / (TR * lax.axis_size(ROWS))
    part = (jnp.sum(part.astype(F32), axis=0) * scale).astype(BF16)
    part = lax.all_to_all(copies_of(part, depth), "z", 0, 0, tiled=True).reshape(SLOT, 128)
    (copies,) = call(
        copies_kernel, (shape((plane, SLOT, 128), BF16),), part,
        scratch=[pltpu.SemaphoreType.DMA((plane,))],
        far_outs=1,
    )
    copies, lefts = lax.optimization_barrier((copies, lefts))
    half = lax.all_to_all(copies, PLANE, 0, 0, tiled=True)
    side = shape((TR, ZCH), BF16)
    to_left, to_right = call(side_kernel, (side, side), lefts, rights, from_above, from_below)
    from_left, from_right = to_neighbours(COLS, to_right, to_left)
    half, from_left, from_right = lax.optimization_barrier((half, from_left, from_right))
    grad_features, grad_hidden = call(
        sum_kernel,
        (shape((TR, TC, FEAT), BF16), shape((TR, TC, CH), BF16)),
        inner, from_above, from_below, from_left, from_right,
    )
    other = lax.ppermute(half, "core", swap)
    outs = (shape((3 * TAPS, GATES), BF16), shape((1, GATES), F32))
    tails = pltpu.VMEM((2, 16, 128), BF16)
    sems = pltpu.SemaphoreType.DMA((2 * GROUPS + 3,))
    grad_kernel, own_bias = call(
        join_own_kernel, outs, half, scratch=[tails, sems], far=1, far_outs=1
    )
    other, grad_features, grad_hidden = lax.optimization_barrier(
        (other, grad_features, grad_hidden)
    )
    grad_kernel, grad_bias = call(
        join_other_kernel, outs, own_bias, other, grad_kernel,
        scratch=[tails, pltpu.VMEM((1, GATES), F32), sems],
        far=2, far_outs=2, aliases={2: 0},
    )
    return (
        hidden_new,
        cell_new,
        grad_features,
        grad_hidden,
        grad_cell,
        grad_kernel.reshape(3, 3, ZCH, GATES),
        grad_bias.reshape(GATES),
    )


def solution(mesh):
    grid = Mesh(mesh.devices.reshape(16, 2, 4, 2, 2), ROWS + COLS)
    tile = P(ROWS, COLS, None)
    return jax.shard_map(
        local,
        mesh=grid,
        in_specs=(tile, tile, tile, P(), P(), tile, tile),
        out_specs=(tile, tile, tile, tile, tile, P(), P()),
        check_vma=False,
    )
```

```python
import jax
import jax.numpy as jnp
from jax import lax
from jax.experimental import pallas as pl
from jax.experimental.pallas import tpu as pltpu
from jax.sharding import Mesh, PartitionSpec as P

ROWS = ("z", "xh")
COLS = ("y", "xl", "core")
PLANE = ("y", "xl", "xh")
BF16 = jnp.bfloat16
F32 = jnp.float32
TR, TC = 8, 64
CELLS = TR * TC
FEAT, CH, ZCH, GATES = 64, 128, 192, 512
TAPS = 3 * ZCH
GROUPS, SLOT = 8, 224
VMEM = 40 * 1024 * 1024


def to_neighbours(axes, last, first):
    count = lax.axis_size(axes)
    inner = [(i, i ^ 1) for i in range(count)]
    outer = [(i, i + 1 if i % 2 else i - 1) for i in range(1, count - 1)]
    even = lax.axis_index(axes[-1]) == 0
    near = lax.ppermute(jnp.where(even, last, first), axes, inner)
    far = lax.ppermute(jnp.where(even, first, last), axes, outer)
    return jnp.where(even, far, near), jnp.where(even, near, far)


def halo_rows(block):
    return to_neighbours(ROWS, block[TR - 1 :], block[:1])


def halo_cols(low, block, high):
    last = jnp.concatenate([low[:, TC - 1 :], block[:, TC - 1 :], high[:, TC - 1 :]], axis=0)
    first = jnp.concatenate([low[:, :1], block[:, :1], high[:, :1]], axis=0)
    return to_neighbours(COLS, last, first)


def shifted(row, before, after):
    place = lax.broadcasted_iota(jnp.int32, row.shape, 0)
    down = jnp.where(place == 0, before, pltpu.roll(row, 1, 0))
    up = jnp.where(place == TC - 1, after, pltpu.roll(row, TC - 1, 0))
    return down, up


def taps_kernel(stacked, taps):
    for r in range(TR):
        row = stacked[r].astype(F32)
        down, up = shifted(row, 0.0, 0.0)
        taps[(r + 1) * TC : (r + 2) * TC, :] = jnp.concatenate([down, row, up], axis=1).astype(BF16)


def half_products(taps, half_gates, half_bias, store, finish=lambda slot: None):
    for a in range(3):
        term = lax.dot_general(
            taps[a * TC : a * TC + CELLS, :],
            half_gates,
            (((0,), (0,)), ((), ())),
            preferred_element_type=F32,
        )
        begin = a * TAPS
        while begin < (a + 1) * TAPS:
            end = min((begin // SLOT + 1) * SLOT, (a + 1) * TAPS)
            group, top = begin // SLOT, begin % SLOT
            for j in range(2):
                block = term[begin - a * TAPS : end - a * TAPS, j * 128 : (j + 1) * 128]
                store(j * GROUPS + group, top, top + end - begin, block)
                if end % SLOT == 0:
                    finish(j * GROUPS + group)
            begin = end
    top = 3 * TAPS - (GROUPS - 1) * SLOT
    for j in range(2):
        slot = j * GROUPS + GROUPS - 1
        row = half_bias[:, j * 128 : (j + 1) * 128]
        store(slot, top, top + 16, jnp.concatenate([row, row], axis=0))
        store(slot, top + 16, SLOT, jnp.zeros((SLOT - top - 16, 128), F32))
        finish(slot)


def cell_kernel(
    own_taps, low, high, left, right, kernel, cell_prev, hidden_cot, cell_cot, bias,
    hidden_out, cell_out, grad_cell_out, grad_gates, taps, sums, send,
    gates, hidden_new, cell_new, grad_cell, sent,
):
    for r, halo in ((0, low), (TR + 1, high)):
        row = halo[0].astype(F32)
        down, up = shifted(row, left[r].astype(F32), right[r].astype(F32))
        taps[r * TC : (r + 1) * TC, :] = jnp.concatenate([down, row, up], axis=1).astype(BF16)
    place = lax.broadcasted_iota(jnp.int32, (16, ZCH), 0)
    for r in range(1, TR + 1):
        begin, end = r * TC, (r + 1) * TC
        taps[begin + 16 : end - 16, :] = own_taps[begin + 16 : end - 16, :]
        block = own_taps[begin : begin + 16, :].astype(F32)
        side = jnp.where(place == 0, left[r].astype(F32), block[:, :ZCH])
        taps[begin : begin + 16, :] = jnp.concatenate([side, block[:, ZCH:]], axis=1).astype(BF16)
        block = own_taps[end - 16 : end, :].astype(F32)
        side = jnp.where(place == 15, right[r].astype(F32), block[:, 2 * ZCH :])
        taps[end - 16 : end, :] = jnp.concatenate([block[:, : 2 * ZCH], side], axis=1).astype(BF16)
    wide = jnp.concatenate([taps[a * TC : a * TC + CELLS, :] for a in range(3)], axis=1)
    weights = kernel[...].reshape(3 * TAPS, GATES)
    total = jnp.dot(wide, weights, preferred_element_type=F32)
    gates[...] = total + bias[...]
    bias_sum = jnp.zeros((8, GATES), F32)
    for r in range(TR):
        rows = slice(r * TC, (r + 1) * TC)
        in_gate = jax.nn.sigmoid(gates[rows, 0:CH])
        forget = jax.nn.sigmoid(gates[rows, CH : 2 * CH])
        out_gate = jax.nn.sigmoid(gates[rows, 2 * CH : 3 * CH])
        cand = jnp.tanh(gates[rows, 3 * CH :])
        before = cell_prev[r]
        new = forget * before + in_gate * cand
        squash = jnp.tanh(new)
        cell_new[r] = new
        hidden_new[r] = (out_gate * squash).astype(BF16)
        hid_cot = hidden_cot[r].astype(F32)
        total = cell_cot[r] + hid_cot * out_gate * (1.0 - squash * squash)
        grad_cell[r] = total * forget
        parts = [
            total * cand * in_gate * (1.0 - in_gate),
            total * before * forget * (1.0 - forget),
            hid_cot * squash * out_gate * (1.0 - out_gate),
            total * in_gate * (1.0 - cand * cand),
        ]
        rounded = jnp.concatenate([part.astype(BF16) for part in parts], axis=1)
        grad_gates[rows, :] = rounded
        wide = rounded.astype(F32).reshape(TC // 8, 8, GATES)
        bias_sum = bias_sum + jnp.sum(wide, axis=0)
    copies = [
        pltpu.make_async_copy(source, target, sent.at[i])
        for i, (source, target) in enumerate(
            ((hidden_new, hidden_out), (cell_new, cell_out), (grad_cell, grad_cell_out))
        )
    ]
    for copy in copies:
        copy.start()
    sums[...] = jnp.broadcast_to(jnp.sum(bias_sum, axis=0, keepdims=True), (8, GATES))
    columns = pl.ds(pl.multiple_of((1 - lax.axis_index("core")) * 256, 256), 256)

    def store(slot, top, end, block):
        send[slot, top:end, :] = block.astype(BF16)

    half_products(taps, grad_gates[:, columns], sums[:, columns], store)
    for copy in copies:
        copy.wait()


def own_kernel(taps, grad_gates, sums, received, result, total, sent):
    columns = pl.ds(pl.multiple_of(lax.axis_index("core") * 256, 256), 256)

    def store(slot, top, end, block):
        total[slot, top:end, :] = (block + received[slot, top:end, :].astype(F32)).astype(BF16)

    def copy(slot):
        return pltpu.make_async_copy(total.at[slot], result.at[slot], sent.at[slot])

    half_products(
        taps, grad_gates[:, columns], sums[:, columns], store, lambda slot: copy(slot).start()
    )
    for slot in range(2 * GROUPS):
        copy(slot).wait()


def input_kernel(grad_gates, kernel, inner, to_above, to_below, lefts, rights, spread):
    spread[...] = jnp.zeros_like(spread)
    for a in range(3):
        spread[a * TC : a * TC + CELLS, :] += lax.dot_general(
            grad_gates[...], kernel[a], (((1,), (1,)), ((), ())), preferred_element_type=F32
        )
    sides = []
    for r in range(TR + 2):
        rows = spread[r * TC : (r + 1) * TC, :]
        lower, middle, upper = rows[:, :ZCH], rows[:, ZCH : 2 * ZCH], rows[:, 2 * ZCH :]
        _, from_lower = shifted(lower, 0.0, 0.0)
        from_upper, _ = shifted(upper, 0.0, 0.0)
        total = middle + from_lower + from_upper
        if 0 < r < TR + 1:
            inner[(r - 1) * TC : r * TC, :] = total
            sides.append((lower[:1], upper[TC - 1 :]))
        else:
            target = to_above if r == 0 else to_below
            corners = [lower[:1], upper[TC - 1 :], jnp.zeros((14, ZCH), F32)]
            target[0:TC, :] = total.astype(BF16)
            target[TC : TC + 16, :] = jnp.concatenate(corners, axis=0).astype(BF16)
    lefts[...] = jnp.concatenate([left for left, _ in sides], axis=0)
    rights[...] = jnp.concatenate([right for _, right in sides], axis=0)


def side_kernel(lefts, rights, from_above, from_below, to_left, to_right):
    place = lax.broadcasted_iota(jnp.int32, (TR, ZCH), 0)
    above = from_above[TC : TC + 16, :].astype(F32)
    below = from_below[TC : TC + 16, :].astype(F32)
    for i, own, target in ((0, lefts, to_left), (1, rights, to_right)):
        extra = jnp.where(place == 0, above[i : i + 1], 0.0)
        extra += jnp.where(place == TR - 1, below[i : i + 1], 0.0)
        target[...] = (own[...] + extra).astype(BF16)


def sum_kernel(
    inner, from_above, from_below, from_left, from_right, grad_features, grad_hidden
):
    before, after = from_left[...].astype(F32), from_right[...].astype(F32)
    place = lax.broadcasted_iota(jnp.int32, (TC, ZCH), 0)
    for r in range(TR):
        row = inner[r * TC : (r + 1) * TC, :]
        row += jnp.where(place == 0, before[r : r + 1], 0.0)
        row += jnp.where(place == TC - 1, after[r : r + 1], 0.0)
        if r == 0:
            row += from_above[0:TC, :].astype(F32)
        if r == TR - 1:
            row += from_below[0:TC, :].astype(F32)
        grad_features[r] = row[:, :FEAT].astype(BF16)
        grad_hidden[r] = row[:, FEAT:].astype(BF16)


def plane_sum_kernel(parts, total):
    result = parts[0].astype(F32)
    for i in range(1, parts.shape[0]):
        result += parts[i].astype(F32)
    total[...] = result.astype(BF16)


def copies_kernel(part, copies, sems):
    moves = [
        pltpu.make_async_copy(part, copies.at[i], sems.at[i]) for i in range(copies.shape[0])
    ]
    for move in moves:
        move.start()
    for move in moves:
        move.wait()


def place_half(slots, place, grad_kernel, last_slots, sems):
    last = 3 * TAPS - (GROUPS - 1) * SLOT
    heads, copies = [], []
    for j in range(2):
        columns = pl.ds(pl.multiple_of(place * 256 + j * 128, 128), 128)
        slot = j * GROUPS + GROUPS - 1
        heads.append(
            pltpu.make_async_copy(
                slots.at[slot, last : last + 16, :], last_slots.at[j], sems.at[2 * GROUPS + j]
            )
        )
        for i in range(GROUPS):
            count = SLOT if i < GROUPS - 1 else last
            copies.append(
                pltpu.make_async_copy(
                    slots.at[j * GROUPS + i, 0:count, :],
                    grad_kernel.at[i * SLOT : i * SLOT + count, columns],
                    sems.at[j * GROUPS + i],
                )
            )
    for copy in heads + copies:
        copy.start()
    for copy in heads:
        copy.wait()
    return [last_slots[j].astype(F32)[0:1] for j in range(2)], copies


def join_own_kernel(slots, grad_kernel, own_bias, last_slots, sems):
    core = lax.axis_index("core")
    rows, copies = place_half(slots, core, grad_kernel, last_slots, sems)
    own_bias[...] = jnp.zeros_like(own_bias)
    for j in range(2):
        own_bias[:, pl.ds(pl.multiple_of(core * 256 + j * 128, 128), 128)] = rows[j]
    for copy in copies:
        copy.wait()


def join_other_kernel(
    own_bias, slots, own_kernel_part, grad_kernel, grad_bias, last_slots, bias, sems
):
    place = 1 - lax.axis_index("core")
    rows, copies = place_half(slots, place, grad_kernel, last_slots, sems)
    bias[...] = own_bias[...]
    for j in range(2):
        bias[:, pl.ds(pl.multiple_of(place * 256 + j * 128, 128), 128)] = rows[j]
    copies.append(pltpu.make_async_copy(bias, grad_bias, sems.at[2 * GROUPS + 2]))
    copies[-1].start()
    for copy in copies:
        copy.wait()


def call(body, outs, *args, scratch=(), flops=0, far=0, far_outs=0, aliases=()):
    moved = sum(x.size * x.dtype.itemsize for x in list(args) + list(outs))
    whole = pl.BlockSpec(memory_space=pltpu.VMEM)
    anywhere = pl.BlockSpec(memory_space=pl.ANY)
    return pl.pallas_call(
        body,
        out_shape=outs,
        in_specs=[whole] * (len(args) - far) + [anywhere] * far,
        out_specs=[anywhere] * far_outs + [whole] * (len(outs) - far_outs),
        input_output_aliases=dict(aliases),
        scratch_shapes=list(scratch),
        cost_estimate=pl.CostEstimate(flops=flops, bytes_accessed=moved, transcendentals=0),
        compiler_params=pltpu.CompilerParams(vmem_limit_bytes=VMEM),
    )(*args)


def copies_of(part, count):
    return lax.optimization_barrier(jnp.broadcast_to(part[None], (count,) + part.shape))


def local(features, hidden_prev, cell_prev, kernel, bias, hidden_cot, cell_cot):
    shape = jax.ShapeDtypeStruct
    work = 2 * CELLS * 3 * TAPS * GATES
    plane = lax.axis_size(PLANE)
    depth = lax.axis_size("z")
    swap = [(0, 1), (1, 0)]
    weights = kernel.reshape(3, TAPS, GATES)

    stacked = jnp.concatenate([features, hidden_prev], axis=2)
    low, high = halo_rows(stacked)
    (own_taps,) = call(
        taps_kernel, (shape(((TR + 2) * TC, TAPS), BF16),), stacked, flops=work
    )
    low, high, own_taps = lax.optimization_barrier((low, high, own_taps))
    left, right = halo_cols(low, stacked, high)
    hidden_new, cell_new, grad_cell, grad_gates, taps, sums, send = call(
        cell_kernel,
        (
            shape((TR, TC, CH), BF16),
            shape((TR, TC, CH), F32),
            shape((TR, TC, CH), F32),
            shape((CELLS, GATES), BF16),
            shape(((TR + 2) * TC, TAPS), BF16),
            shape((8, GATES), F32),
            shape((plane, SLOT, 128), BF16),
        ),
        own_taps, low, high, left, right, weights, cell_prev, hidden_cot, cell_cot,
        bias.reshape(1, GATES),
        scratch=[
            pltpu.VMEM((CELLS, GATES), F32),
            pltpu.VMEM((TR, TC, CH), BF16),
            pltpu.VMEM((TR, TC, CH), F32),
            pltpu.VMEM((TR, TC, CH), F32),
            pltpu.SemaphoreType.DMA((3,)),
        ],
        flops=work + work // 2,
        far_outs=3,
    )
    received = lax.ppermute(send, "core", swap)
    inner, to_above, to_below, lefts, rights = call(
        input_kernel,
        (
            shape((CELLS, ZCH), F32),
            shape((TC + 16, ZCH), BF16),
            shape((TC + 16, ZCH), BF16),
            shape((TR, ZCH), F32),
            shape((TR, ZCH), F32),
        ),
        grad_gates, weights,
        scratch=[pltpu.VMEM(((TR + 2) * TC, TAPS), F32)],
        flops=work,
    )
    received, to_above, to_below = lax.optimization_barrier((received, to_above, to_below))
    (half,) = call(
        own_kernel, (shape((plane, SLOT, 128), BF16),), taps, grad_gates, sums, received,
        scratch=[pltpu.VMEM((plane, SLOT, 128), BF16), pltpu.SemaphoreType.DMA((plane,))],
        flops=work // 2,
        far_outs=1,
    )
    half, to_above, to_below = lax.optimization_barrier((half, to_above, to_below))
    part = lax.all_to_all(half, PLANE, 0, 0, tiled=True)
    from_above, from_below = to_neighbours(ROWS, to_below, to_above)
    part, from_above, from_below = lax.optimization_barrier((part, from_above, from_below))
    (part,) = call(plane_sum_kernel, (shape((SLOT, 128), BF16),), part)
    part = lax.all_to_all(part.reshape(depth, SLOT // depth, 128), "z", 0, 0, tiled=True)
    scale = 1.0 / (TR * lax.axis_size(ROWS))
    part = (jnp.sum(part.astype(F32), axis=0) * scale).astype(BF16)
    part = lax.all_to_all(copies_of(part, depth), "z", 0, 0, tiled=True).reshape(SLOT, 128)
    (copies,) = call(
        copies_kernel, (shape((plane, SLOT, 128), BF16),), part,
        scratch=[pltpu.SemaphoreType.DMA((plane,))],
        far_outs=1,
    )
    copies, lefts = lax.optimization_barrier((copies, lefts))
    half = lax.all_to_all(copies, PLANE, 0, 0, tiled=True)
    side = shape((TR, ZCH), BF16)
    to_left, to_right = call(side_kernel, (side, side), lefts, rights, from_above, from_below)
    from_left, from_right = to_neighbours(COLS, to_right, to_left)
    half, from_left, from_right = lax.optimization_barrier((half, from_left, from_right))
    grad_features, grad_hidden = call(
        sum_kernel,
        (shape((TR, TC, FEAT), BF16), shape((TR, TC, CH), BF16)),
        inner, from_above, from_below, from_left, from_right,
    )
    other = lax.ppermute(half, "core", swap)
    outs = (shape((3 * TAPS, GATES), BF16), shape((1, GATES), F32))
    tails = pltpu.VMEM((2, 16, 128), BF16)
    sems = pltpu.SemaphoreType.DMA((2 * GROUPS + 3,))
    grad_kernel, own_bias = call(
        join_own_kernel, outs, half, scratch=[tails, sems], far=1, far_outs=1
    )
    other, grad_features, grad_hidden = lax.optimization_barrier(
        (other, grad_features, grad_hidden)
    )
    grad_kernel, grad_bias = call(
        join_other_kernel, outs, own_bias, other, grad_kernel,
        scratch=[tails, pltpu.VMEM((1, GATES), F32), sems],
        far=2, far_outs=2, aliases={2: 0},
    )
    return (
        hidden_new,
        cell_new,
        grad_features,
        grad_hidden,
        grad_cell,
        grad_kernel.reshape(3, 3, ZCH, GATES),
        grad_bias.reshape(GATES),
    )


def solution(mesh):
    grid = Mesh(mesh.devices.reshape(16, 2, 4, 2, 2), ROWS + COLS)
    tile = P(ROWS, COLS, None)
    return jax.shard_map(
        local,
        mesh=grid,
        in_specs=(tile, tile, tile, P(), P(), tile, tile),
        out_specs=(tile, tile, tile, tile, tile, P(), P()),
        check_vma=False,
    )
```
